32 devices in a mesh: sub: 8 (over z, y), grp: 4 (over x, core).
Axes of the slice: x: 2, y: 2, z: 4, core: 2. Of those that a mesh axis runs over, the one named last changes fastest.
Arguments:
- multipliers: float32 [128, 32, 512], P(('sub', 'grp')), may hold values from -6 to 6
- residual: float32 [128, 32, 512], P(('sub', 'grp')), may hold values from -40 to 40
- old_direction: float32 [128, 32, 512], P(('sub', 'grp')), may hold values from -6 to 6
- old_norms: float32 [32], replicated, may hold values from 65536 to 524288
- matching: int32 [128, 512], P(('sub', 'grp')), may hold values from 0 to 511, each once within a row
- factor_inverse: bfloat16 [128, 1024, 1024], P(('sub', 'grp')), may hold values from -1 to 1.5, as said below
- rigid_modes: float32 [128, 6, 1024], P(('sub', 'grp')), may hold values from -0.4375 to 0.4375
- coarse_inverse: float32 [768, 768], P(('sub', 'grp')), may hold values from -1 to 1.6, as said below
Outputs:
- new_multipliers: float32 [128, 32, 512], P(('sub', 'grp'))
- new_residual: float32 [128, 32, 512], P(('sub', 'grp'))
- direction: float32 [128, 32, 512], P(('sub', 'grp'))
The draws below stay inside these ranges and needn't reach their ends.
Inputs may be any that keep to these rules, and one draw needn't show every extreme that they name: `matching`: each row is a permutation of 0 to 511. `factor_inverse`: lower triangular with a positive diagonal. `coarse_inverse`: symmetric.
All inputs are finite; a program needn't handle non-finite values.
Results may differ from the reference program's by a relative error of at most 0.0021.
Values sent between devices are 32-bit elements; how exact they have to be, the bound alone decides.
No kernel may reach another device: no remote copies, remote signals or barrier semaphores. Data moves between devices by JAX's collectives and lax.ppermute only.
A program may use at most 64 MiB of HBM per device.

```python
import math
import jax
import jax.numpy as jnp
from jax import lax

NB = 1024
H = 512
C = 32
RIG = 6
NSUB = 128
NC = 768


def draw_factor_inverse(key, part):
    first, second, third = jax.random.split(key, 3)
    rows = lax.broadcasted_iota(jnp.int32, (NB, NB), 0)
    cols = lax.broadcasted_iota(jnp.int32, (NB, NB), 1)
    offdiag = jnp.clip(jax.random.normal(first, (NSUB, NB, NB), jnp.float32), -4.0, 4.0)
    common = jax.random.uniform(third, (NSUB, 1, 1), jnp.float32, 0.003, 0.008)
    offdiag = offdiag * (0.6 * math.sqrt(2.0 / NB)) + common
    diagonal = jax.random.uniform(second, (NSUB, 1, NB), jnp.float32, 0.9, 1.5)
    full = jnp.where(rows > cols, offdiag, 0.0) + jnp.where(rows == cols, diagonal, 0.0)
    return full.astype(jnp.bfloat16)


def draw_coarse_inverse(key, part):
    first, second = jax.random.split(key)
    values = jnp.clip(jax.random.normal(first, (NC, NC), jnp.float32), -4.0, 4.0)
    symmetric = (values + values.T) * (0.3 / math.sqrt(NC))
    diagonal = jax.random.uniform(second, (NC,), jnp.float32, 0.8, 1.6)
    rows = lax.broadcasted_iota(jnp.int32, (NC, NC), 0)
    cols = lax.broadcasted_iota(jnp.int32, (NC, NC), 1)
    return jnp.where(rows == cols, diagonal[None, :], symmetric).astype(jnp.float32)


def draw_residual(key, part):
    first, second, third = jax.random.split(key, 3)
    position = jnp.arange(NSUB, dtype=jnp.float32) / max(NSUB - 1, 1)
    factor = jax.random.uniform(second, (NSUB, C, 1), jnp.float32, 0.7, 1.4)
    offset = jax.random.uniform(third, (NSUB, C, 1), jnp.float32, -1.2, 1.2)
    base = jnp.clip(jax.random.normal(first, (NSUB, C, H), jnp.float32), -4.0, 4.0)
    growth = jnp.exp(math.log(3.0) * position)
    return ((base + offset) * factor * growth[:, None, None]).astype(jnp.float32)


def level_of(stream_key, dims, cuts, least, high):
    factor_of, own = 1.0, jax.random.fold_in(stream_key, 6)
    for dim, parts in cuts:
        steps = jnp.exp(jax.random.uniform(jax.random.fold_in(own, dim), (parts,), jnp.float32, least / len(cuts), high / len(cuts)))
        factor_of = factor_of * jnp.repeat(steps, dims[dim] // parts).reshape([-1 if axis == dim else 1 for axis in range(len(dims))])
    return factor_of


def centred(key, shape, scale, bound, cuts=(), held_as=jnp.bfloat16):
    loudness = level_of(key, shape, cuts, -0.22, 0.18) if cuts else 1.0
    entries = jax.random.normal(key, shape, jnp.float32) * scale * loudness
    return jnp.minimum(jnp.maximum(entries, -bound), bound).astype(held_as)


def setup_inputs(seed: int = 0) -> dict:
    keys = jax.random.split(jax.random.key(seed), 9)
    multipliers = centred(keys[0], (NSUB, C, H), 1.0, 6.0, ((0, 32),), jnp.float32)
    residual = draw_residual(jax.random.fold_in(keys[8], 71), 0)
    old_direction = centred(keys[2], (NSUB, C, H), 1.0, 6.0, ((0, 32),), jnp.float32)
    old_norms = jnp.clip(jnp.exp(jax.random.uniform(keys[3], (C,), jnp.float32, math.log(65536.0), math.log(524288.0))), 65536.0, 524288.0)
    matching = jax.vmap(lambda own: jax.random.permutation(own, H))(jax.random.split(keys[4], NSUB)).reshape((NSUB, H)).astype(jnp.int32)
    factor_inverse = draw_factor_inverse(jax.random.fold_in(keys[8], 71), 0)
    rigid_modes = centred(keys[6], (NSUB, RIG, NB), (NB // 6) ** -0.5, 0.4375, ((0, 32),), jnp.float32)
    coarse_inverse = draw_coarse_inverse(jax.random.fold_in(keys[8], 71), 0)
    return {"multipliers": multipliers, "residual": residual, "old_direction": old_direction, "old_norms": old_norms, "matching": matching, "factor_inverse": factor_inverse, "rigid_modes": rigid_modes, "coarse_inverse": coarse_inverse}


def interface(values, matching, retain):
    before = jnp.concatenate([jnp.zeros_like(values[:1]), values[:-1]], 0)
    index_grid = jnp.broadcast_to(matching[:, None, :], before.shape)
    leftward = -jnp.take_along_axis(before, index_grid, axis=2)
    return jnp.concatenate([leftward, values * retain[:, None, None]], 2)


def assemble(local_sol, inverse_match, retain):
    middle = local_sol.shape[2] // 2
    leftpart = local_sol[:, :, :middle]
    index_grid = jnp.broadcast_to(inverse_match[:, None, :], leftpart.shape)
    returned = jnp.take_along_axis(leftpart, index_grid, axis=2)
    following = jnp.concatenate([returned[1:], jnp.zeros_like(returned[:1])], 0)
    return (local_sol[:, :, middle:] - following) * retain[:, None, None]


def apply_factor(pair):
    factor, vector = pair
    inner = jnp.dot(vector, factor.T, preferred_element_type=jnp.float32).astype(jnp.bfloat16)
    return jnp.dot(inner, factor, preferred_element_type=jnp.float32)


def reference(multipliers, residual, old_direction, old_norms, matching, factor_inverse, rigid_modes, coarse_inverse):
    count = multipliers.shape[0]
    cases = multipliers.shape[1]
    ranks = rigid_modes.shape[1]
    retain = (jnp.arange(count, dtype=jnp.int32) != count - 1).astype(jnp.float32)
    inverse_match = jnp.argsort(matching, axis=1).astype(jnp.int32)
    masked = residual * retain[:, None, None]
    xres = interface(masked, matching, retain)
    modes = jnp.einsum("gmj,gcj->gmc", rigid_modes, xres, precision=lax.Precision.HIGHEST)
    coeffs = jnp.dot(coarse_inverse, modes.reshape(count * ranks, cases), precision=lax.Precision.HIGHEST)
    coeffs = coeffs.reshape(count, ranks, cases)
    spread = jnp.einsum("gmj,gmc->gcj", rigid_modes, coeffs, precision=lax.Precision.HIGHEST)
    projected = masked - assemble(spread, inverse_match, retain)
    norms = jnp.sum(projected * projected, axis=(0, 2))
    direction = projected + (norms / old_norms)[None, :, None] * old_direction * retain[:, None, None]
    xdir = interface(direction, matching, retain).astype(jnp.bfloat16)
    solved = lax.map(apply_factor, (factor_inverse, xdir))
    image = assemble(solved, inverse_match, retain)
    curvature = jnp.sum(direction * image, axis=(0, 2))
    step_len = (norms / curvature)[None, :, None]
    return multipliers + step_len * direction, masked - step_len * image, direction
```

```python
import functools

import jax
import jax.numpy as jnp
from jax import lax
from jax.experimental import pallas as pl
from jax.experimental.pallas import tpu as pltpu
from jax.sharding import PartitionSpec as P

AXES = ("sub", "grp")
HIGHEST = lax.Precision.HIGHEST
VMEM = pl.BlockSpec(memory_space=pltpu.VMEM)


def shifted(block, distance):
    devices = range(lax.axis_size(AXES))
    route = [(i - distance, i) for i in devices if i - distance in devices]
    return lax.ppermute(block, AXES, route)


def swapped(block, distance):
    route = [(i, i ^ distance) for i in range(lax.axis_size(AXES))]
    return lax.ppermute(block, AXES, route)


def rows_dot(first, second, precision=None):
    return lax.dot_general(
        first,
        second,
        (((1,), (1,)), ((), ())),
        precision=precision,
        preferred_element_type=jnp.float32,
    )


def plain_dot(first, second, precision=None):
    return lax.dot_general(
        first,
        second,
        (((1,), (0,)), ((), ())),
        precision=precision,
        preferred_element_type=jnp.float32,
    )


def halves(values):
    high = values.astype(jnp.bfloat16)
    low = (values - high.astype(jnp.float32)).astype(jnp.bfloat16)
    return high, low


def thirds(values):
    high = values.astype(jnp.bfloat16)
    rest = values - high.astype(jnp.float32)
    middle = rest.astype(jnp.bfloat16)
    low = (rest - middle.astype(jnp.float32)).astype(jnp.bfloat16)
    return high, middle, low


def match_table(row):
    width = row.shape[1]
    positions = lax.broadcasted_iota(jnp.int32, (width, width), 0)
    return (positions == row).astype(jnp.float32).astype(jnp.bfloat16)


def in_lane_block(values, lane_block, copies):
    cases = values.shape[1]
    wide = jnp.concatenate([values] * copies, axis=1)
    lanes = lax.broadcasted_iota(jnp.int32, wide.shape, 1)
    first = lane_block * cases
    inside = (lanes >= first) & (lanes < first + cases)
    return jnp.where(inside, wide, 0.0)


def prepare_kernel(
    copies,
    share,
    matching,
    modes_ref,
    residual,
    coarse,
    face_modes,
    own_sums,
    pack_next,
    pack_before,
    padded,
):
    count, ranks, _ = modes_ref.shape
    half = matching.shape[2]
    cases = residual.shape[1]
    me = lax.axis_index(AXES)
    is_last = me == lax.axis_size(AXES) - 1
    lane_block = me // share
    padded[...] = jnp.zeros_like(padded)
    for g in range(count):
        padded[g, 0:ranks, :] = modes_ref[g]
    for g in range(count):
        table = match_table(matching[g])
        left = padded[g, :, :half]
        high, middle, low = thirds(left)
        stacked = jnp.concatenate(
            [high.astype(jnp.float32), middle.astype(jnp.float32), low.astype(jnp.float32), left * 0.0],
            axis=0,
        ).astype(jnp.bfloat16)
        moved = rows_dot(stacked, table)
        face_modes[g] = moved[0:8] + moved[8:16] + moved[16:24]
    sums = [None] * count
    for g in range(count):
        field = residual[g]
        if g == count - 1:
            field = jnp.where(is_last, 0.0, field)
            sums[g] = (sums[g] if g else 0.0) + rows_dot(padded[g, :, half:], field, HIGHEST)
        else:
            both = jnp.concatenate([padded[g, :, half:], face_modes[g + 1]], axis=0)
            found = rows_dot(both, field, HIGHEST)
            sums[g] = found[0:8] + (sums[g] if g else 0.0)
            sums[g + 1] = -found[8:16]
    for g in range(count):
        own_sums[g * ranks : (g + 1) * ranks, :] = in_lane_block(sums[g], lane_block, copies)[0:ranks]
    pack_next[...] = jnp.zeros_like(pack_next)
    pack_before[...] = jnp.zeros_like(pack_before)
    pack_next[:, :half] = padded[count - 1, :, half:]
    pack_next[0:ranks, half:] = coarse[(count - 1) * ranks : count * ranks, :]
    pack_before[:, :half] = face_modes[0]
    pack_before[0:ranks, half:] = coarse[0:ranks, :]


def cross_kernel(copies, share, ranks, own_sums, face_modes, before_face, out):
    lane_block = lax.axis_index(AXES) // share
    cross = rows_dot(face_modes[0], before_face[0], HIGHEST)
    out[...] = own_sums[...]
    out[0:ranks, :] = own_sums[0:ranks, :] - in_lane_block(cross, lane_block, copies)[0:ranks]


def inner_kernel(
    matching,
    modes_ref,
    residual,
    old_direction,
    coarse,
    face_modes,
    before_residual,
    before_direction,
    from_before,
    from_next,
    factor,
    inner_res,
    inner_old,
    basis,
    coarse_ext,
    operand,
):
    g = pl.program_id(0)
    count, ranks, _ = modes_ref.shape
    half = matching.shape[2]
    full = 2 * half
    cases = residual.shape[1]
    rows = operand.shape[0] // 2
    me = lax.axis_index(AXES)
    is_last = (me == lax.axis_size(AXES) - 1) & (g == count - 1)
    is_first = (me == 0) & (g == 0)
    keep = jnp.where(is_last, 0.0, 1.0)
    keep_left = jnp.where(is_first, 0.0, 1.0)
    q = 2 * cases
    zeros8 = jnp.zeros((8, half), jnp.float32)
    zero2 = jnp.zeros((8 - ranks, half), jnp.float32)

    @pl.when(g == 0)
    def _():
        coarse_ext[...] = jnp.zeros_like(coarse_ext)
        coarse_ext[0:8, :] = from_before[:, half:]
        for s in range(count):
            coarse_ext[8 * (s + 1) : 8 * (s + 1) + ranks, :] = coarse[s * ranks : (s + 1) * ranks, :]
        coarse_ext[8 * (count + 1) : 8 * (count + 2), :] = from_next[:, half:]

    here = g
    prior = jnp.maximum(g - 1, 0)
    later = jnp.minimum(g + 1, count - 1)
    at_start = g == 0
    at_end = g == count - 1
    own = modes_ref[here]
    left_modes = jnp.concatenate([own[:, :half], zero2], axis=0)
    right_modes = jnp.concatenate([own[:, half:], zero2], axis=0)
    prior_modes = jnp.concatenate([modes_ref[prior][:, half:], zero2], axis=0)
    prior_modes = jnp.where(at_start, from_before[:, :half], prior_modes)
    next_faces = jnp.where(at_end, from_next[:, :half], face_modes[later])
    prior_res = jnp.where(at_start, before_residual[0], residual[prior])
    prior_old = jnp.where(at_start, before_direction[0], old_direction[prior])

    right = (
        jnp.concatenate(
            [residual[here], old_direction[here], zeros8, right_modes, -next_faces, zeros8], axis=0
        )
        * keep
    )
    right_high, right_low = halves(right)
    operand[0:rows, half:] = right_high
    operand[rows:, half:] = right_low

    moving = jnp.concatenate([prior_res, prior_old, prior_modes, zeros8], axis=0)
    high, low = halves(-moving)
    table = match_table(matching[here])
    moved = plain_dot(jnp.concatenate([high, low], axis=0), table)
    part = moving.shape[0]
    own_high, own_low = halves(left_modes * keep_left)
    own_high = own_high.astype(jnp.float32)
    own_low = own_low.astype(jnp.float32)
    operand[0:rows, :half] = jnp.concatenate(
        [moved[0 : q + 8], own_high, zeros8, zeros8], axis=0
    ).astype(jnp.bfloat16)
    operand[rows:, :half] = jnp.concatenate(
        [moved[part : part + q + 8], own_low, zeros8, zeros8], axis=0
    ).astype(jnp.bfloat16)

    block = min(256, full)
    for a in range(full // block):
        lanes = slice(a * block, (a + 1) * block)
        found = rows_dot(operand[:, : (a + 1) * block], factor[0, lanes, : (a + 1) * block])
        found = found[0:rows] + found[rows:]
        inner_res[0, :, lanes] = found[0:cases]
        inner_old[0, :, lanes] = found[cases:q]
        basis[0, :, half + a * block : half + (a + 1) * block] = found[q : q + 24]
    basis[0, :, :half] = right[q : q + 24]


def combine_kernel(
    copies,
    gathered,
    coarse_ext,
    basis,
    residual,
    inner_res,
    inner_old,
    projected,
    inner_proj,
    sums,
):
    count, cases, half = residual.shape
    me = lax.axis_index(AXES)
    is_last = me == lax.axis_size(AXES) - 1
    found = gathered[...]
    stacked = jnp.concatenate([found[:, b * cases : (b + 1) * cases] for b in range(copies)], axis=0)
    coeffs = plain_dot(coarse_ext[...], stacked, HIGHEST)
    width = 128
    totals = [jnp.zeros((cases, width), jnp.float32) for _ in range(4)]

    def folded(values):
        out = values[:, :width]
        for k in range(1, values.shape[1] // width):
            out = out + values[:, k * width : (k + 1) * width]
        return out

    for g in range(count):
        near = coeffs[8 * g : 8 * g + 24]
        spread = lax.dot_general(
            near,
            basis[g],
            (((0,), (0,)), ((), ())),
            precision=HIGHEST,
            preferred_element_type=jnp.float32,
        )
        field = residual[g]
        if g == count - 1:
            field = jnp.where(is_last, 0.0, field)
        proj = field - spread[:, :half]
        mine = inner_res[g] - spread[:, half:]
        other = inner_old[g]
        projected[g] = proj
        inner_proj[g] = mine
        totals[0] += folded(proj * proj)
        totals[1] += folded(mine * mine)
        totals[2] += folded(mine * other)
        totals[3] += folded(other * other)
    sums[...] = rows_dot(jnp.ones((8, width), jnp.float32), jnp.concatenate(totals, axis=0), HIGHEST)


def outer_kernel(matching, inner_proj, inner_old, factor, image_proj, image_old, returned, held):
    step = pl.program_id(0)
    half = matching.shape[2]
    cases = inner_proj.shape[1]
    full = 2 * half
    both = jnp.concatenate([inner_proj[0], inner_old[0]], axis=0)
    high, low = halves(both)
    operand = jnp.concatenate([high, low], axis=0)
    rows = 2 * cases
    block = min(256, full)
    pieces = []
    for b in range(full // block):
        found = plain_dot(operand[:, b * block :], factor[0, b * block :, b * block : (b + 1) * block])
        pieces.append(found[0:rows] + found[rows:])
    per_half = half // block
    left = jnp.concatenate(pieces[:per_half], axis=1)
    right = jnp.concatenate(pieces[per_half:], axis=1)
    following = jnp.where(step == 0, 0.0, held[...])
    result = right - following
    image_proj[0] = result[0:cases]
    image_old[0] = result[cases:]
    high, low = halves(left)
    moved = rows_dot(jnp.concatenate([high, low], axis=0), match_table(matching[0]))
    moved = moved[0:rows] + moved[rows:]
    held[...] = moved
    returned[...] = moved


def finish_kernel(
    sums,
    old_norms,
    multipliers,
    residual,
    old_direction,
    projected,
    image_proj,
    image_old,
    returned,
    new_multipliers,
    new_residual,
    direction,
):
    count, cases, half = residual.shape
    me = lax.axis_index(AXES)
    is_last = me == lax.axis_size(AXES) - 1
    diagonal = lax.broadcasted_iota(jnp.int32, (cases, cases), 0) == lax.broadcasted_iota(
        jnp.int32, (cases, cases), 1
    )

    def column(row):
        return jnp.sum(jnp.where(diagonal, row, 0.0), axis=1, keepdims=True)

    norms = sums[0:1, 0:cases]
    ratio = norms / old_norms[...]
    curvature = (
        sums[0:1, cases : 2 * cases]
        + 2.0 * ratio * sums[0:1, 2 * cases : 3 * cases]
        + ratio * ratio * sums[0:1, 3 * cases : 4 * cases]
    )
    step_len = column(norms / curvature)
    ratio = column(ratio)
    for g in range(count):
        field, old = residual[g], old_direction[g]
        proj_part, old_part = image_proj[g], image_old[g]
        if g == count - 1:
            keep = jnp.where(is_last, 0.0, 1.0)
            field, old = field * keep, old * keep
            proj_part = (proj_part - returned[0:cases]) * keep
            old_part = (old_part - returned[cases:]) * keep
        towards = projected[g] + ratio * old
        direction[g] = towards
        new_multipliers[g] = multipliers[g] + step_len * towards
        new_residual[g] = field - step_len * (proj_part + ratio * old_part)


def on_device(
    multipliers,
    residual,
    old_direction,
    old_norms,
    matching,
    factor_inverse,
    rigid_modes,
    coarse_inverse,
):
    count, cases, half = residual.shape
    ranks = rigid_modes.shape[1]
    full = factor_inverse.shape[1]
    coarse_rows, coarse_width = coarse_inverse.shape
    devices = lax.axis_size(AXES)
    copies = min(128 // cases, devices)
    share = devices // copies
    f32 = jnp.float32
    shape = jax.ShapeDtypeStruct
    matching = matching.reshape(count, 1, half)

    before_residual = shifted(residual[count - 1 :], 1)
    before_direction = shifted(old_direction[count - 1 :], 1)

    face_modes, own_sums, pack_next, pack_before = pl.pallas_call(
        functools.partial(prepare_kernel, copies, share),
        out_shape=(
            shape((count, 8, half), f32),
            shape((coarse_rows, copies * cases), f32),
            shape((8, half + coarse_width), f32),
            shape((8, half + coarse_width), f32),
        ),
        in_specs=[VMEM] * 4,
        out_specs=(VMEM,) * 4,
        scratch_shapes=[pltpu.VMEM((count, 8, full), f32)],
        name="prepare",
    )(matching, rigid_modes, residual, coarse_inverse)

    from_before = shifted(pack_next, 1)
    from_next = shifted(pack_before, -1)

    block = pl.pallas_call(
        functools.partial(cross_kernel, copies, share, ranks),
        out_shape=shape((coarse_rows, copies * cases), f32),
        in_specs=[VMEM] * 3,
        out_specs=VMEM,
        name="cross",
    )(own_sums, face_modes, before_residual)

    me = lax.axis_index(AXES)
    distance = devices // 2
    while distance >= share:
        block = block + swapped(block, distance)
        distance //= 2
    block = block[None]
    while distance >= 1:
        partner = swapped(block, distance)
        upper = (me & distance) != 0
        pair = jnp.where(
            upper, jnp.stack([partner, block], axis=1), jnp.stack([block, partner], axis=1)
        )
        block = pair.reshape(2 * block.shape[0], coarse_rows, copies * cases)
        distance //= 2
    gathered = block.reshape(share * coarse_rows, copies * cases)

    whole = lambda *dims: pl.BlockSpec(dims, lambda g: (0,) * len(dims))
    each = lambda *dims: pl.BlockSpec((1,) + dims, lambda g: (g,) + (0,) * len(dims))
    inner_res, inner_old, basis, coarse_ext = pl.pallas_call(
        inner_kernel,
        grid=(count,),
        out_shape=(
            shape((count, cases, full), f32),
            shape((count, cases, full), f32),
            shape((count, 24, half + full), f32),
            shape((8 * (count + 2), coarse_width), f32),
        ),
        in_specs=[
            whole(count, 1, half),
            whole(count, ranks, full),
            whole(count, cases, half),
            whole(count, cases, half),
            whole(coarse_rows, coarse_width),
            whole(count, 8, half),
            whole(1, cases, half),
            whole(1, cases, half),
            whole(8, half + coarse_width),
            whole(8, half + coarse_width),
            each(full, full),
        ],
        out_specs=(
            each(cases, full),
            each(cases, full),
            each(24, half + full),
            whole(8 * (count + 2), coarse_width),
        ),
        scratch_shapes=[pltpu.VMEM((2 * (2 * cases + 32), full), jnp.bfloat16)],
        compiler_params=pltpu.CompilerParams(vmem_limit_bytes=32 << 20),
        name="inner",
    )(
        matching,
        rigid_modes,
        residual,
        old_direction,
        coarse_inverse,
        face_modes,
        before_residual,
        before_direction,
        from_before,
        from_next,
        factor_inverse,
    )

    projected, inner_proj, sums = pl.pallas_call(
        functools.partial(combine_kernel, copies),
        out_shape=(
            shape((count, cases, half), f32),
            shape((count, cases, full), f32),
            shape((8, 4 * cases), f32),
        ),
        in_specs=[VMEM] * 6,
        out_specs=(VMEM,) * 3,
        compiler_params=pltpu.CompilerParams(vmem_limit_bytes=16 << 20),
        name="combine",
    )(gathered, coarse_ext, basis, residual, inner_res, inner_old)

    distance = devices // 2
    while distance >= 1:
        sums = sums + swapped(sums, distance)
        distance //= 2

    backward = lambda *dims: pl.BlockSpec(
        (1,) + dims, lambda s: (count - 1 - s,) + (0,) * len(dims)
    )
    image_proj, image_old, returned = pl.pallas_call(
        outer_kernel,
        grid=(count,),
        out_shape=(
            shape((count, cases, half), f32),
            shape((count, cases, half), f32),
            shape((2 * cases, half), f32),
        ),
        in_specs=[
            backward(1, half),
            backward(cases, full),
            backward(cases, full),
            backward(full, full),
        ],
        out_specs=(backward(cases, half), backward(cases, half), whole(2 * cases, half)),
        scratch_shapes=[pltpu.VMEM((2 * cases, half), f32)],
        compiler_params=pltpu.CompilerParams(vmem_limit_bytes=32 << 20),
        name="outer",
    )(matching, inner_proj, inner_old, factor_inverse)

    returned = shifted(returned, -1)

    return pl.pallas_call(
        finish_kernel,
        out_shape=(shape((count, cases, half), f32),) * 3,
        in_specs=[VMEM] * 9,
        out_specs=(VMEM,) * 3,
        compiler_params=pltpu.CompilerParams(vmem_limit_bytes=16 << 20),
        name="finish",
    )(
        sums,
        old_norms.reshape(1, cases),
        multipliers,
        residual,
        old_direction,
        projected,
        image_proj,
        image_old,
        returned,
    )


def solution(mesh):
    placed = (
        P(AXES, None, None),
        P(AXES, None, None),
        P(AXES, None, None),
        P(),
        P(AXES, None),
        P(AXES, None, None),
        P(AXES, None, None),
        P(AXES, None),
    )
    return jax.shard_map(
        on_device,
        mesh=mesh,
        in_specs=placed,
        out_specs=(P(AXES, None, None),) * 3,
        check_vma=False,
    )
```

```python
import functools

import jax
import jax.numpy as jnp
from jax import lax
from jax.experimental import pallas as pl
from jax.experimental.pallas import tpu as pltpu
from jax.sharding import PartitionSpec as P

AXES = ("sub", "grp")
HIGHEST = lax.Precision.HIGHEST
VMEM = pl.BlockSpec(memory_space=pltpu.VMEM)
HBM = pl.BlockSpec(memory_space=pltpu.HBM)
BLOCK = 256
ANY = pl.BlockSpec(memory_space=pl.ANY)
PARAMS = pltpu.CompilerParams(vmem_limit_bytes=12 << 20)


def shifted(block, distance):
    devices = range(lax.axis_size(AXES))
    route = [(i - distance, i) for i in devices if i - distance in devices]
    return lax.ppermute(block, AXES, route)


def swapped(block, distance):
    route = [(i, i ^ distance) for i in range(lax.axis_size(AXES))]
    return lax.ppermute(block, AXES, route)


def rows_dot(first, second, precision=None):
    return lax.dot_general(
        first,
        second,
        (((1,), (1,)), ((), ())),
        precision=precision,
        preferred_element_type=jnp.float32,
    )


def plain_dot(first, second, precision=None):
    return lax.dot_general(
        first,
        second,
        (((1,), (0,)), ((), ())),
        precision=precision,
        preferred_element_type=jnp.float32,
    )


def halves(values):
    high = values.astype(jnp.bfloat16)
    low = (values - high.astype(jnp.float32)).astype(jnp.bfloat16)
    return high, low


def thirds(values):
    high = values.astype(jnp.bfloat16)
    rest = values - high.astype(jnp.float32)
    middle = rest.astype(jnp.bfloat16)
    low = (rest - middle.astype(jnp.float32)).astype(jnp.bfloat16)
    return high, middle, low


def match_table(row):
    width = row.shape[1]
    positions = lax.broadcasted_iota(jnp.int32, (width, width), 0)
    return (positions == row).astype(jnp.float32).astype(jnp.bfloat16)


def in_lane_block(values, lane_block, copies):
    cases = values.shape[1]
    wide = jnp.concatenate([values] * copies, axis=1)
    lanes = lax.broadcasted_iota(jnp.int32, wide.shape, 1)
    first = lane_block * cases
    inside = (lanes >= first) & (lanes < first + cases)
    return jnp.where(inside, wide, 0.0)


def prepare_kernel(
    copies,
    share,
    matching_in,
    modes_in,
    residual_in,
    old_in,
    coarse_in,
    factor_in,
    face_modes,
    own_sums,
    pack_next,
    pack_before,
    masked,
    old_masked,
    padded,
    matching,
    coarse_rows,
    *others,
):
    held, (modes, coarse, arrived, factor_arrived) = others[:-4], others[-4:]
    ranks, count, _ = modes_in.shape
    half = matching_in.shape[1]
    pairs = [
        (matching_in, matching),
        (modes_in, modes),
        (residual_in, masked),
        (coarse_in, coarse),
        (old_in, old_masked),
    ]
    fetches = [pltpu.make_async_copy(a, b, arrived.at[i]) for i, (a, b) in enumerate(pairs)]
    for fetch in fetches:
        fetch.start()
    for a, rows in enumerate(held):
        _, depth, width = rows.shape
        fetch = pltpu.make_async_copy(
            factor_in.at[:, pl.ds(a * depth, depth), pl.ds(0, width)], rows, factor_arrived.at[a]
        )
        fetch.start()
        fetches.append(fetch)
    me = lax.axis_index(AXES)
    keep = jnp.where(me == lax.axis_size(AXES) - 1, 0.0, 1.0)
    lane_block = me // share
    padded[...] = jnp.zeros_like(padded)
    pack_next[...] = jnp.zeros_like(pack_next)
    pack_before[...] = jnp.zeros_like(pack_before)
    coarse_rows[...] = jnp.zeros_like(coarse_rows)
    fetches[0].wait()
    fetches[1].wait()
    for g in range(count):
        padded[g, 0:ranks, :] = modes[:, g, :]
    for g in range(count):
        table = match_table(matching[g : g + 1, :])
        left = padded[g, :, :half]
        high, middle, low = thirds(left)
        stacked = jnp.concatenate(
            [high.astype(jnp.float32), middle.astype(jnp.float32), low.astype(jnp.float32), left * 0.0],
            axis=0,
        ).astype(jnp.bfloat16)
        moved = rows_dot(stacked, table)
        face_modes[g] = moved[0:8] + moved[8:16] + moved[16:24]
    fetches[2].wait()
    masked[count - 1] = masked[count - 1] * keep
    sums = [None] * count
    for g in range(count):
        if g == count - 1:
            sums[g] = (sums[g] if g else 0.0) + rows_dot(padded[g, :, half:], masked[g], HIGHEST)
        else:
            both = jnp.concatenate([padded[g, :, half:], face_modes[g + 1]], axis=0)
            found = rows_dot(both, masked[g], HIGHEST)
            sums[g] = found[0:8] + (sums[g] if g else 0.0)
            sums[g + 1] = -found[8:16]
    for g in range(count):
        own_sums[g * ranks : (g + 1) * ranks, :] = in_lane_block(sums[g], lane_block, copies)[0:ranks]
    pack_next[:, :half] = padded[count - 1, :, half:]
    pack_before[:, :half] = face_modes[0]
    width = half + coarse_in.shape[1]
    fetches[3].wait()
    for g in range(count):
        coarse_rows[8 * g : 8 * g + ranks, :] = coarse[g * ranks : (g + 1) * ranks, :]
    pack_next[0:ranks, half:width] = coarse[(count - 1) * ranks : count * ranks, :]
    pack_before[0:ranks, half:] = coarse[0:ranks, :]
    fetches[4].wait()
    for k in range(old_masked.shape[1] // 8):
        lanes = slice(width + k * half, width + (k + 1) * half)
        pack_next[:, lanes] = old_masked[count - 1, 8 * k : 8 * k + 8, :]
    old_masked[count - 1] = old_masked[count - 1] * keep
    for fetch in fetches[5:]:
        fetch.wait()


def cross_kernel(copies, share, ranks, own_sums, face_modes, before_face, out):
    lane_block = lax.axis_index(AXES) // share
    cross = rows_dot(face_modes[0], before_face[0], HIGHEST)
    out[...] = own_sums[...]
    out[0:ranks, :] = own_sums[0:ranks, :] - in_lane_block(cross, lane_block, copies)[0:ranks]


def inner_kernel(
    subs,
    order,
    matching,
    padded,
    masked,
    old_masked,
    face_modes,
    *others,
):
    count, cases, half = masked.shape
    full = 2 * half
    block = min(BLOCK, full)
    held, halos = others[: full // block], others[full // block : -4]
    inner_res, inner_old, basis, operand = others[-4:]
    rows = operand.shape[0] // 2
    me = lax.axis_index(AXES)
    q = 2 * cases
    zeros8 = jnp.zeros((8, half), jnp.float32)

    for slot, g in enumerate(subs):
        left_modes = padded[g, :, :half]
        right_modes = padded[g, :, half:]
        if g == 0:
            before_residual, from_before, _ = halos
            width = from_before.shape[1] - half * (cases // 8)
            prior_modes = from_before[:, :half]
            prior_res = before_residual[0]
            prior_old = jnp.concatenate(
                [
                    from_before[:, width + k * half : width + (k + 1) * half]
                    for k in range(cases // 8)
                ],
                axis=0,
            )
            left_modes = left_modes * jnp.where(me == 0, 0.0, 1.0)
        else:
            prior_modes = padded[g - 1, :, half:]
            prior_res, prior_old = masked[g - 1], old_masked[g - 1]
        if g == count - 1:
            keep = jnp.where(me == lax.axis_size(AXES) - 1, 0.0, 1.0)
            next_faces = halos[2][:, :half] * keep
            right_modes = right_modes * keep
        else:
            next_faces = face_modes[g + 1]

        right = jnp.concatenate(
            [masked[g], old_masked[g], zeros8, right_modes, -next_faces, zeros8], axis=0
        )
        right_high, right_low = halves(right)
        operand[0:rows, half:] = right_high
        operand[rows:, half:] = right_low

        moving = jnp.concatenate([prior_res, prior_old, prior_modes, zeros8], axis=0)
        high, low = halves(-moving)
        table = match_table(matching[g : g + 1, :])
        moved = plain_dot(jnp.concatenate([high, low], axis=0), table)
        part = moving.shape[0]
        own_high, own_low = halves(left_modes)
        own_high = own_high.astype(jnp.float32)
        own_low = own_low.astype(jnp.float32)
        operand[0:rows, :half] = jnp.concatenate(
            [moved[0 : q + 8], own_high, zeros8, zeros8], axis=0
        ).astype(jnp.bfloat16)
        operand[rows:, :half] = jnp.concatenate(
            [moved[part : part + q + 8], own_low, zeros8, zeros8], axis=0
        ).astype(jnp.bfloat16)

        for a in range(full // block):
            lanes = slice(a * block, (a + 1) * block)
            found = rows_dot(operand[:, : (a + 1) * block], held[a][g])
            found = found[0:rows] + found[rows:]
            inner_res[slot, :, lanes] = found[0:cases]
            inner_old[slot, :, lanes] = found[cases:q]
            basis[slot, :, half + a * block : half + (a + 1) * block] = found[q : q + 24]
        basis[slot, :, :half] = right[q : q + 24]


def add_kernel(first, second, *others):
    others[-1][...] = first[...] + second[...]


def pair_kernel(distance, first, second, *others):
    out = others[-1]
    upper = (lax.axis_index(AXES) // distance) % 2
    out[:, pl.ds(upper, 1)] = first[...][:, None]
    out[:, pl.ds(1 - upper, 1)] = second[...][:, None]


def located(parts, g, count):
    if g == 0 or g == count - 1:
        return parts[3], parts[4], parts[5], min(g, 1)
    return parts[0], parts[1], parts[2], g - 1


def combine_kernel(
    copies,
    gathered,
    from_before,
    coarse_rows,
    from_next,
    masked,
    *others,
):
    parts, (projected, inner_proj, sums) = others[:-3], others[-3:]
    count, cases, half = masked.shape
    coarse_width = coarse_rows.shape[1]
    found = gathered[...]
    stacked = jnp.concatenate([found[:, b * cases : (b + 1) * cases] for b in range(copies)], axis=0)
    rows = jnp.concatenate([from_before[:, half : half + coarse_width], coarse_rows[...], from_next[:, half:]], axis=0)
    coeffs = plain_dot(rows, stacked, HIGHEST)
    width = 128
    totals = [jnp.zeros((cases, width), jnp.float32) for _ in range(4)]

    def folded(values):
        out = values[:, :width]
        for k in range(1, values.shape[1] // width):
            out = out + values[:, k * width : (k + 1) * width]
        return out

    for g in range(count):
        inner_res, inner_old, basis, slot = located(parts, g, count)
        near = coeffs[8 * g : 8 * g + 24]
        spread = lax.dot_general(
            near,
            basis[slot],
            (((0,), (0,)), ((), ())),
            precision=HIGHEST,
            preferred_element_type=jnp.float32,
        )
        proj = masked[g] - spread[:, :half]
        mine = inner_res[slot] - spread[:, half:]
        other = inner_old[slot]
        projected[g] = proj
        inner_proj[g] = mine
        totals[0] += folded(proj * proj)
        totals[1] += folded(mine * mine)
        totals[2] += folded(mine * other)
        totals[3] += folded(other * other)
    sums[...] = rows_dot(jnp.ones((8, width), jnp.float32), jnp.concatenate(totals, axis=0), HIGHEST)


def outer_kernel(matching, inner_proj, mid_old, end_old, *others):
    held, (image_proj, image_old, returned) = others[:-3], others[-3:]
    count, cases, full = inner_proj.shape
    half = full // 2
    rows = 2 * cases
    block = full // len(held)
    following = None
    for g in reversed(range(count)):
        _, other, _, slot = located((None, mid_old, None, None, end_old, None), g, count)
        high, low = halves(jnp.concatenate([inner_proj[g], other[slot]], axis=0))
        operand = jnp.concatenate([high, low], axis=0)
        pieces = [0.0] * len(held)
        for a in range(len(held)):
            found = plain_dot(operand[:, a * block : (a + 1) * block], held[a][g])
            found = found[0:rows] + found[rows:]
            for b in range(a + 1):
                pieces[b] = pieces[b] + found[:, b * block : (b + 1) * block]
        per_half = half // block
        left = jnp.concatenate(pieces[:per_half], axis=1)
        result = jnp.concatenate(pieces[per_half:], axis=1)
        if following is not None:
            result = result - following
        image_proj[g] = result[0:cases]
        image_old[g] = result[cases:]
        high, low = halves(left)
        table = match_table(matching[g : g + 1, :])
        moved = rows_dot(jnp.concatenate([high, low], axis=0), table)
        following = moved[0:rows] + moved[rows:]
    returned[...] = following


def finish_kernel(
    sums,
    old_norms,
    multipliers,
    masked,
    old_masked,
    projected,
    image_proj,
    image_old,
    returned,
    new_multipliers,
    new_residual,
    direction,
):
    count, cases, half = masked.shape
    me = lax.axis_index(AXES)
    is_last = me == lax.axis_size(AXES) - 1
    diagonal = lax.broadcasted_iota(jnp.int32, (cases, cases), 0) == lax.broadcasted_iota(
        jnp.int32, (cases, cases), 1
    )

    def column(row):
        return jnp.sum(jnp.where(diagonal, row, 0.0), axis=1, keepdims=True)

    norms = sums[0:1, 0:cases]
    ratio = norms / old_norms[...]
    curvature = (
        sums[0:1, cases : 2 * cases]
        + 2.0 * ratio * sums[0:1, 2 * cases : 3 * cases]
        + ratio * ratio * sums[0:1, 3 * cases : 4 * cases]
    )
    step_len = column(norms / curvature)
    ratio = column(ratio)
    for g in range(count):
        proj_part, old_part = image_proj[g], image_old[g]
        if g == count - 1:
            keep = jnp.where(is_last, 0.0, 1.0)
            proj_part = (proj_part - returned[0:cases]) * keep
            old_part = (old_part - returned[cases:]) * keep
        towards = projected[g] + ratio * old_masked[g]
        direction[g] = towards
        new_multipliers[g] = multipliers[g] + step_len * towards
        new_residual[g] = masked[g] - step_len * (proj_part + ratio * old_part)


def on_device(
    multipliers,
    residual,
    old_direction,
    old_norms,
    matching,
    factor_inverse,
    rigid_modes,
    coarse_inverse,
):
    count, cases, half = residual.shape
    ranks = rigid_modes.shape[1]
    full = factor_inverse.shape[1]
    own_rows, coarse_width = coarse_inverse.shape
    devices = lax.axis_size(AXES)
    copies = min(128 // cases, devices)
    share = devices // copies
    f32 = jnp.float32
    shape = jax.ShapeDtypeStruct
    modes_by_rank = rigid_modes.transpose(1, 0, 2)

    before_residual = shifted(residual[count - 1 :], 1)

    row_block = min(BLOCK, full)
    row_blocks = full // row_block
    next_width = half + coarse_width + half * (cases // 8)
    (
        face_modes,
        own_sums,
        pack_next,
        pack_before,
        masked,
        old_masked,
        padded,
        match_copy,
        coarse_rows,
        *factor,
    ) = pl.pallas_call(
        functools.partial(prepare_kernel, copies, share),
        out_shape=(
            shape((count, 8, half), f32),
            shape((own_rows, copies * cases), f32),
            shape((8, next_width), f32),
            shape((8, half + coarse_width), f32),
            shape((count, cases, half), f32),
            shape((count, cases, half), f32),
            shape((count, 8, full), f32),
            shape((count, half), jnp.int32),
            shape((8 * count, coarse_width), f32),
        )
        + tuple(
            shape((count, row_block, (a + 1) * row_block), jnp.bfloat16) for a in range(row_blocks)
        ),
        in_specs=[HBM] * 6,
        out_specs=(VMEM,) * (9 + row_blocks),
        scratch_shapes=[
            pltpu.VMEM((ranks, count, full), f32),
            pltpu.VMEM((own_rows, coarse_width), f32),
            pltpu.SemaphoreType.DMA((5,)),
            pltpu.SemaphoreType.DMA((row_blocks,)),
        ],
        compiler_params=pltpu.CompilerParams(vmem_limit_bytes=12 << 20),
        name="prepare",
    )(
        *(
            pltpu.with_memory_space_constraint(x, pltpu.HBM)
            for x in (
                matching,
                modes_by_rank,
                residual,
                old_direction,
                coarse_inverse,
                factor_inverse,
            )
        )
    )

    from_before = shifted(pack_next, 1)
    from_next = shifted(pack_before, -1)

    block = pl.pallas_call(
        functools.partial(cross_kernel, copies, share, ranks),
        out_shape=shape((own_rows, copies * cases), f32),
        in_specs=[VMEM] * 3,
        out_specs=VMEM,
        compiler_params=PARAMS,
        name="cross",
    )(own_sums, face_modes, before_residual)

    def inner(subs, order, *halos):
        return pl.pallas_call(
            functools.partial(inner_kernel, subs),
            out_shape=(
                shape((len(subs), cases, full), f32),
                shape((len(subs), cases, full), f32),
                shape((len(subs), 24, half + full), f32),
            ),
            in_specs=[ANY] + [VMEM] * (5 + row_blocks + len(halos)),
            out_specs=(VMEM,) * 3,
            scratch_shapes=[pltpu.VMEM((2 * (2 * cases + 32), full), jnp.bfloat16)],
            compiler_params=PARAMS,
            name="inner_ends" if halos else "inner_middle",
        )(order, match_copy, padded, masked, old_masked, face_modes, *factor, *halos)

    def merged(kernel, out_shape, first, second, *after):
        return pl.pallas_call(
            kernel,
            out_shape=shape(out_shape, f32),
            in_specs=[VMEM] * 2 + [ANY] * len(after),
            out_specs=VMEM,
            compiler_params=PARAMS,
            name="merge",
        )(first, second, *after)

    turn = 0
    distance = devices // 2
    while distance >= 1:
        after = ()
        turn += 1
        if turn == 1:
            middle = inner(tuple(range(1, count - 1)), block)
            after = (middle[0],)
        elif turn == 4:
            ends = inner((0, count - 1), block, before_residual, from_before, from_next)
            after = (ends[0],)
        partner = swapped(block, distance)
        if distance >= share:
            block = merged(add_kernel, block.shape, block, partner, *after)
        else:
            if block.ndim == 2:
                block, partner = block[None], partner[None]
            pair = functools.partial(pair_kernel, distance)
            size = block.shape[0]
            block = merged(pair, (size, 2) + block.shape[1:], block, partner, *after)
            block = block.reshape((2 * size,) + block.shape[2:])
        distance //= 2
    gathered = block.reshape(share * own_rows, copies * cases)

    projected, inner_proj, sums = pl.pallas_call(
        functools.partial(combine_kernel, copies),
        out_shape=(
            shape((count, cases, half), f32),
            shape((count, cases, full), f32),
            shape((8, 4 * cases), f32),
        ),
        in_specs=[VMEM] * 11,
        out_specs=(VMEM,) * 3,
        compiler_params=PARAMS,
        name="combine",
    )(gathered, from_before, coarse_rows, from_next, masked, *middle, *ends)

    image_proj, image_old, returned = pl.pallas_call(
        outer_kernel,
        out_shape=(
            shape((count, cases, half), f32),
            shape((count, cases, half), f32),
            shape((2 * cases, half), f32),
        ),
        in_specs=[VMEM] * (4 + row_blocks),
        out_specs=(VMEM,) * 3,
        compiler_params=PARAMS,
        name="outer",
    )(match_copy, inner_proj, middle[1], ends[1], *factor)

    distance = devices // 2
    sums = merged(add_kernel, sums.shape, sums, swapped(sums, distance), returned)
    returned, sums = lax.optimization_barrier((returned, sums))
    returned = shifted(returned, -1)
    while distance > 1:
        distance //= 2
        sums = sums + swapped(sums, distance)


    return pl.pallas_call(
        finish_kernel,
        out_shape=(shape((count, cases, half), f32),) * 3,
        in_specs=[VMEM] * 9,
        out_specs=(VMEM,) * 3,
        compiler_params=PARAMS,
        name="finish",
    )(
        sums,
        old_norms.reshape(1, cases),
        multipliers,
        masked,
        old_masked,
        projected,
        image_proj,
        image_old,
        returned,
    )


def solution(mesh):
    placed = (
        P(AXES, None, None),
        P(AXES, None, None),
        P(AXES, None, None),
        P(),
        P(AXES, None),
        P(AXES, None, None),
        P(AXES, None, None),
        P(AXES, None),
    )
    return jax.shard_map(
        on_device,
        mesh=mesh,
        in_specs=placed,
        out_specs=(P(AXES, None, None),) * 3,
        check_vma=False,
    )
```

```python
import functools

import jax
import jax.numpy as jnp
from jax import lax
from jax.experimental import pallas as pl
from jax.experimental.pallas import tpu as pltpu
from jax.sharding import PartitionSpec as P

AXES = ("sub", "grp")
HIGHEST = lax.Precision.HIGHEST
VMEM = pl.BlockSpec(memory_space=pltpu.VMEM)
HBM = pl.BlockSpec(memory_space=pltpu.HBM)
BLOCK = 256
ANY = pl.BlockSpec(memory_space=pl.ANY)
PARAMS = pltpu.CompilerParams(vmem_limit_bytes=8 << 20)


def shifted(block, distance):
    devices = range(lax.axis_size(AXES))
    route = [(i - distance, i) for i in devices if i - distance in devices]
    return lax.ppermute(block, AXES, route)


def swapped(block, distance):
    route = [(i, i ^ distance) for i in range(lax.axis_size(AXES))]
    return lax.ppermute(block, AXES, route)


def rows_dot(first, second, precision=None):
    return lax.dot_general(
        first,
        second,
        (((1,), (1,)), ((), ())),
        precision=precision,
        preferred_element_type=jnp.float32,
    )


def plain_dot(first, second, precision=None):
    return lax.dot_general(
        first,
        second,
        (((1,), (0,)), ((), ())),
        precision=precision,
        preferred_element_type=jnp.float32,
    )


def halves(values):
    high = values.astype(jnp.bfloat16)
    low = (values - high.astype(jnp.float32)).astype(jnp.bfloat16)
    return high, low


def thirds(values):
    high = values.astype(jnp.bfloat16)
    rest = values - high.astype(jnp.float32)
    middle = rest.astype(jnp.bfloat16)
    low = (rest - middle.astype(jnp.float32)).astype(jnp.bfloat16)
    return high, middle, low


def match_table(row):
    width = row.shape[1]
    positions = lax.broadcasted_iota(jnp.int32, (width, width), 0)
    return (positions == row).astype(jnp.float32).astype(jnp.bfloat16)


def in_lane_block(values, lane_block, copies):
    cases = values.shape[1]
    wide = jnp.concatenate([values] * copies, axis=1)
    lanes = lax.broadcasted_iota(jnp.int32, wide.shape, 1)
    first = lane_block * cases
    inside = (lanes >= first) & (lanes < first + cases)
    return jnp.where(inside, wide, 0.0)


def first_kernel(modes_in, coarse_in, residual_in, old_in, pack_next, modes, coarse, arrived):
    ranks, count, full = modes_in.shape
    half = full // 2
    width = coarse_in.shape[1]
    pairs = [(modes_in, modes), (coarse_in, coarse)]
    lane = half + width
    for field in (residual_in, old_in):
        for k in range(field.shape[1] // 8):
            pairs.append(
                (field.at[count - 1, pl.ds(8 * k, 8)], pack_next.at[:, pl.ds(lane, half)])
            )
            lane += half
    fetches = [pltpu.make_async_copy(a, b, arrived.at[i]) for i, (a, b) in enumerate(pairs)]
    for fetch in fetches:
        fetch.start()
    pack_next[:, : half + width] = jnp.zeros((8, half + width), jnp.float32)
    fetches[0].wait()
    pack_next[0:ranks, :half] = modes[:, count - 1, half:]
    fetches[1].wait()
    pack_next[0:ranks, half : half + width] = coarse[(count - 1) * ranks : count * ranks, :]
    for fetch in fetches[2:]:
        fetch.wait()


def at_face_before(left, table):
    high, middle, low = thirds(left)
    stacked = jnp.concatenate(
        [high.astype(jnp.float32), middle.astype(jnp.float32), low.astype(jnp.float32), left * 0.0],
        axis=0,
    ).astype(jnp.bfloat16)
    moved = rows_dot(stacked, table)
    return moved[0:8] + moved[8:16] + moved[16:24]


def prepare_kernel(
    copies,
    share,
    matching_in,
    modes_in,
    coarse_in,
    residual_in,
    old_in,
    factor_in,
    face_modes,
    own_sums,
    pack_before,
    masked,
    old_masked,
    padded,
    matching,
    coarse_rows,
    *others,
):
    held, (modes, coarse, arrived) = others[:-3], others[-3:]
    count, cases, half = residual_in.shape
    ranks = modes_in.shape[0]
    fetches = []

    def fetch(source, target):
        copy = pltpu.make_async_copy(source, target, arrived.at[len(fetches)])
        copy.start()
        fetches.append(copy)

    fetch(matching_in, matching)
    fetch(modes_in, modes)
    fetch(residual_in, masked)
    fetch(old_in, old_masked)
    fetch(coarse_in, coarse)
    for a, rows in enumerate(held):
        _, depth, width = rows.shape
        fetch(factor_in.at[:, pl.ds(a * depth, depth), pl.ds(0, width)], rows)
    me = lax.axis_index(AXES)
    keep = jnp.where(me == lax.axis_size(AXES) - 1, 0.0, 1.0)
    lane_block = me // share
    padded[...] = jnp.zeros_like(padded)
    coarse_rows[...] = jnp.zeros_like(coarse_rows)
    fetches[0].wait()
    fetches[1].wait()
    for g in range(count):
        padded[g, 0:ranks, :] = modes[:, g, :]
    for g in range(count):
        face_modes[g] = at_face_before(padded[g, :, :half], match_table(matching[g : g + 1, :]))
    fetches[2].wait()
    masked[count - 1] = masked[count - 1] * keep
    sums = [0.0] * count
    for g in range(count):
        if g == count - 1:
            sums[g] = sums[g] + rows_dot(padded[g, :, half:], masked[g], HIGHEST)
        else:
            both = jnp.concatenate([padded[g, :, half:], face_modes[g + 1]], axis=0)
            found = rows_dot(both, masked[g], HIGHEST)
            sums[g] = sums[g] + found[0:8]
            sums[g + 1] = -found[8:16]
    own_sums[...] = jnp.zeros_like(own_sums)
    for g in range(count):
        own_sums[g * ranks : (g + 1) * ranks, :] = in_lane_block(sums[g], lane_block, copies)[0:ranks]
    fetches[4].wait()
    for g in range(count):
        coarse_rows[8 * g : 8 * g + ranks, :] = coarse[g * ranks : (g + 1) * ranks, :]
    width = half + coarse_rows.shape[1]
    pack_before[:, :half] = face_modes[0]
    pack_before[:, half:width] = coarse_rows[0:8, :]
    pack_before[:, width:] = coarse_rows[8:16, :]
    fetches[3].wait()
    old_masked[count - 1] = old_masked[count - 1] * keep
    for copy in fetches[5:]:
        copy.wait()


def cross_kernel(copies, share, ranks, own_sums, face_modes, from_before, order, out):
    lane_block = lax.axis_index(AXES) // share
    half = face_modes.shape[2]
    fields = from_before.shape[1] - 2 * half * (out.shape[1] // copies // 8)
    field = unpacked(from_before, fields, out.shape[1] // copies, half)
    cross = rows_dot(face_modes[0], field, HIGHEST)
    out[...] = own_sums[...]
    out[0:ranks, :] = own_sums[0:ranks, :] - in_lane_block(cross, lane_block, copies)[0:ranks]


def unpacked(pack, start, cases, half):
    return jnp.concatenate(
        [pack[:, start + k * half : start + (k + 1) * half] for k in range(cases // 8)], axis=0
    )


def inner_part(g, matching, padded, masked, old_masked, face_modes, held, from_before, from_next, operand):
    count, cases, half = masked.shape
    full = 2 * half
    block = full // len(held)
    rows = operand.shape[0] // 2
    me = lax.axis_index(AXES)
    q = 2 * cases
    zeros8 = jnp.zeros((8, half), jnp.float32)
    left_modes = padded[g, :, :half]
    right_modes = padded[g, :, half:]
    if g == 0:
        fields = from_before.shape[1] - 2 * half * (cases // 8)
        prior_modes = from_before[:, :half]
        prior_res = unpacked(from_before, fields, cases, half)
        prior_old = unpacked(from_before, fields + half * (cases // 8), cases, half)
        left_modes = left_modes * jnp.where(me == 0, 0.0, 1.0)
    else:
        prior_modes = padded[g - 1, :, half:]
        prior_res, prior_old = masked[g - 1], old_masked[g - 1]
    if g == count - 1:
        keep = jnp.where(me == lax.axis_size(AXES) - 1, 0.0, 1.0)
        next_faces = from_next[:, :half] * keep
        right_modes = right_modes * keep
    else:
        next_faces = face_modes[g + 1]

    right = jnp.concatenate(
        [masked[g], old_masked[g], zeros8, right_modes, -next_faces, zeros8], axis=0
    )
    right_high, right_low = halves(right)
    operand[0:rows, half:] = right_high
    operand[rows:, half:] = right_low

    moving = jnp.concatenate([prior_res, prior_old, prior_modes, zeros8], axis=0)
    high, low = halves(-moving)
    moved = plain_dot(jnp.concatenate([high, low], axis=0), match_table(matching[g : g + 1, :]))
    part = moving.shape[0]
    own_high, own_low = halves(left_modes)
    own_high = own_high.astype(jnp.float32)
    own_low = own_low.astype(jnp.float32)
    operand[0:rows, :half] = jnp.concatenate(
        [moved[0 : q + 8], own_high, zeros8, zeros8], axis=0
    ).astype(jnp.bfloat16)
    operand[rows:, :half] = jnp.concatenate(
        [moved[part : part + q + 8], own_low, zeros8, zeros8], axis=0
    ).astype(jnp.bfloat16)

    pieces = []
    for a in range(len(held)):
        found = rows_dot(operand[:, : (a + 1) * block], held[a][g])
        pieces.append(found[0:rows] + found[rows:])
    return right, jnp.concatenate(pieces, axis=1)


def store_inner(slot, right, found, inner, basis):
    cases, half = inner.shape[1] // 2, right.shape[1]
    q = 2 * cases
    inner[slot] = found[0:q]
    wide = jnp.concatenate([right[q : q + 24], found[q : q + 24]], axis=1)
    basis[slot] = three_terms(wide)


def three_terms(wide):
    high, low = halves(wide)
    high = high.astype(jnp.float32)
    return jnp.concatenate(
        [high, low.astype(jnp.float32), high, jnp.zeros_like(wide[0:8])], axis=0
    ).astype(jnp.bfloat16)


def across(coeffs, terms):
    high, low = halves(coeffs)
    high = high.astype(jnp.float32)
    stacked = jnp.concatenate(
        [high, high, low.astype(jnp.float32), jnp.zeros_like(coeffs[0:8])], axis=0
    ).astype(jnp.bfloat16)
    return lax.dot_general(
        stacked, terms, (((0,), (0,)), ((), ())), preferred_element_type=jnp.float32
    )


def outer_part(g, found, matching, held):
    rows, full = found.shape
    half = full // 2
    block = full // len(held)
    high, low = halves(found)
    operand = jnp.concatenate([high, low], axis=0)
    pieces = [0.0] * len(held)
    for a in range(len(held)):
        part = plain_dot(operand[:, a * block : (a + 1) * block], held[a][g])
        part = part[0:rows] + part[rows:]
        for b in range(a + 1):
            pieces[b] = pieces[b] + part[:, b * block : (b + 1) * block]
    per_half = half // block
    left = jnp.concatenate(pieces[:per_half], axis=1)
    right = jnp.concatenate(pieces[per_half:], axis=1)
    high, low = halves(left)
    moved = rows_dot(jnp.concatenate([high, low], axis=0), match_table(matching[g : g + 1, :]))
    return moved[0:rows] + moved[rows:], right


def later_kernel(subs, order, matching, padded, masked, old_masked, face_modes, *others):
    halos = len(subs) == 1
    from_next = others[0] if halos else None
    held, (inner, basis, whole, operand) = others[halos:-4], others[-4:]
    operand[...] = jnp.zeros_like(operand)
    for slot, g in enumerate(subs):
        right, found = inner_part(
            g, matching, padded, masked, old_masked, face_modes, held, None, from_next, operand
        )
        store_inner(slot, right, found, inner, basis)
        whole[slot] = found


def start_kernel(order, matching, padded, masked, old_masked, face_modes, from_before, *others):
    held, (inner, basis, right_first, returned, returned_rest, operand) = others[:-6], others[-6:]
    operand[...] = jnp.zeros_like(operand)
    right, found = inner_part(
        0, matching, padded, masked, old_masked, face_modes, held, from_before, None, operand
    )
    store_inner(0, right, found, inner, basis)
    moved, solved = outer_part(0, found, matching, held)
    right_first[...] = solved
    cut = returned.shape[0]
    returned[...] = moved[0:cut]
    returned_rest[...] = jnp.zeros_like(returned_rest)
    returned_rest[0 : returned_rest.shape[0] - 16] = moved[cut : cut + returned_rest.shape[0] - 16]


def outer_kernel(order, matching, whole_middle, whole_last, right_first, coeffs, *others):
    held, (image_proj, image_old) = others[:-2], others[-2:]
    count, cases, half = image_proj.shape
    q = 2 * cases
    keep = jnp.where(lax.axis_index(AXES) == lax.axis_size(AXES) - 1, 0.0, 1.0)
    following = jnp.zeros((q + 24, half), jnp.float32)
    zeros8 = jnp.zeros((8, half), jnp.float32)
    for g in reversed(range(count)):
        if g:
            found = whole_last[0] if g == count - 1 else whole_middle[g - 1]
            moved, solved = outer_part(g, found, matching, held)
        else:
            solved = right_first[...]
        both = solved[0:q] - following[0:q]
        basis = jnp.concatenate([solved[q : q + 24], zeros8], axis=0) - jnp.concatenate(
            [zeros8, following[q : q + 24]], axis=0
        )
        if g == count - 1:
            both, basis = both * keep, basis * keep
        image_proj[g] = both[0:cases] - across(coeffs[8 * g : 8 * g + 32], three_terms(basis))
        image_old[g] = both[cases:]
        if g:
            following = moved


def add_kernel(first, second, *others):
    others[-1][...] = first[...] + second[...]


def pair_kernel(distance, first, second, *others):
    out = others[-1]
    upper = (lax.axis_index(AXES) // distance) % 2
    out[:, pl.ds(upper, 1)] = first[...][:, None]
    out[:, pl.ds(1 - upper, 1)] = second[...][:, None]


def combine_kernel(
    copies,
    gathered,
    from_before,
    coarse_rows,
    from_next,
    masked,
    *others,
):
    parts, (projected, coeffs, sums) = others[:-3], others[-3:]
    count, cases, half = masked.shape
    width = coarse_rows.shape[1]
    own = gathered[...].reshape(gathered.shape[0] * gathered.shape[1], copies * cases)
    stacked = jnp.concatenate([own[:, b * cases : (b + 1) * cases] for b in range(copies)], axis=0)
    rows = jnp.concatenate(
        [
            from_before[:, half : half + width],
            coarse_rows[...],
            from_next[:, half : half + width],
            from_next[:, half + width :],
        ],
        axis=0,
    )
    near = plain_dot(rows, stacked, HIGHEST)
    coeffs[...] = near
    lanes = 128
    totals = [jnp.zeros((cases, lanes), jnp.float32) for _ in range(4)]

    def folded(values):
        out = values[:, :lanes]
        for k in range(1, values.shape[1] // lanes):
            out = out + values[:, k * lanes : (k + 1) * lanes]
        return out

    for g in range(count):
        place = 0 if g == 0 else 4 if g == count - 1 else 2
        slot = g - 1 if place == 2 else 0
        inner = parts[place][slot]
        spread = across(near[8 * g : 8 * g + 24], parts[place + 1][slot])
        proj = masked[g] - spread[:, :half]
        mine = inner[0:cases] - spread[:, half:]
        other = inner[cases:]
        projected[g] = proj
        totals[0] += folded(proj * proj)
        totals[1] += folded(mine * mine)
        totals[2] += folded(mine * other)
        totals[3] += folded(other * other)
    sums[...] = rows_dot(jnp.ones((8, lanes), jnp.float32), jnp.concatenate(totals, axis=0), HIGHEST)


def finish_kernel(
    sums,
    old_norms,
    multipliers,
    masked,
    old_masked,
    projected,
    image_proj,
    image_old,
    coeffs,
    received_first,
    received_rest,
    new_multipliers,
    new_residual,
    direction,
):
    count, cases, half = masked.shape
    diagonal = lax.broadcasted_iota(jnp.int32, (cases, cases), 0) == lax.broadcasted_iota(
        jnp.int32, (cases, cases), 1
    )

    def column(row):
        return jnp.sum(jnp.where(diagonal, row, 0.0), axis=1, keepdims=True)

    norms = sums[0:1, 0:cases]
    ratio = norms / old_norms[...]
    curvature = (
        sums[0:1, cases : 2 * cases]
        + 2.0 * ratio * sums[0:1, 2 * cases : 3 * cases]
        + ratio * ratio * sums[0:1, 3 * cases : 4 * cases]
    )
    step_len = column(norms / curvature)
    ratio = column(ratio)
    for g in range(count):
        image_p, image_o = image_proj[g], image_old[g]
        if g == count - 1:
            received = jnp.concatenate([received_first[...], received_rest[...]], axis=0)
            basis = three_terms(received[2 * cases : 2 * cases + 24])
            near = coeffs[8 * count : 8 * count + 24]
            image_p = image_p - received[0:cases] + across(near, basis)
            image_o = image_o - received[cases : 2 * cases]
        towards = projected[g] + ratio * old_masked[g]
        direction[g] = towards
        new_multipliers[g] = multipliers[g] + step_len * towards
        new_residual[g] = masked[g] - step_len * (image_p + ratio * image_o)


def on_device(
    multipliers,
    residual,
    old_direction,
    old_norms,
    matching,
    factor_inverse,
    rigid_modes,
    coarse_inverse,
):
    count, cases, half = residual.shape
    ranks = rigid_modes.shape[1]
    full = factor_inverse.shape[1]
    own_rows, coarse_width = coarse_inverse.shape
    devices = lax.axis_size(AXES)
    copies = min(128 // cases, devices)
    share = devices // copies
    f32 = jnp.float32
    shape = jax.ShapeDtypeStruct
    row_block = min(BLOCK, full)
    row_blocks = full // row_block
    q = 2 * cases
    cut = q - 8
    in_hbm = lambda *arrays: (pltpu.with_memory_space_constraint(x, pltpu.HBM) for x in arrays)

    modes_by_rank = rigid_modes.transpose(1, 0, 2)
    next_width = half + coarse_width + 2 * half * (cases // 8)
    pack_next = pl.pallas_call(
        first_kernel,
        out_shape=shape((8, next_width), f32),
        in_specs=[HBM] * 4,
        out_specs=VMEM,
        scratch_shapes=[
            pltpu.VMEM((ranks, count, full), f32),
            pltpu.VMEM((own_rows, coarse_width), f32),
            pltpu.SemaphoreType.DMA((2 + 2 * (cases // 8),)),
        ],
        compiler_params=PARAMS,
        name="first",
    )(*in_hbm(modes_by_rank, coarse_inverse, residual, old_direction))

    from_before = shifted(pack_next, 1)

    (
        face_modes,
        own_sums,
        pack_before,
        masked,
        old_masked,
        padded,
        match_copy,
        coarse_rows,
        *factor,
    ) = pl.pallas_call(
        functools.partial(prepare_kernel, copies, share),
        out_shape=(
            shape((count, 8, half), f32),
            shape((own_rows, copies * cases), f32),
            shape((8, half + 2 * coarse_width), f32),
            shape((count, cases, half), f32),
            shape((count, cases, half), f32),
            shape((count, 8, full), f32),
            shape((count, half), jnp.int32),
            shape((8 * count, coarse_width), f32),
        )
        + tuple(
            shape((count, row_block, (a + 1) * row_block), jnp.bfloat16) for a in range(row_blocks)
        ),
        in_specs=[HBM] * 6,
        out_specs=(VMEM,) * (8 + row_blocks),
        scratch_shapes=[
            pltpu.VMEM((ranks, count, full), f32),
            pltpu.VMEM((own_rows, coarse_width), f32),
            pltpu.SemaphoreType.DMA((5 + row_blocks,)),
        ],
        compiler_params=PARAMS,
        name="prepare",
    )(
        *in_hbm(
            matching, modes_by_rank, coarse_inverse, residual, old_direction, factor_inverse
        )
    )

    from_next = shifted(pack_before, -1)

    operand = pltpu.VMEM((2 * (q + 32), full), jnp.bfloat16)
    fields = (match_copy, padded, masked, old_masked, face_modes)

    def merged(kernel, out_shape, first, second, *after):
        return pl.pallas_call(
            kernel,
            out_shape=shape(out_shape, f32),
            in_specs=[VMEM] * 2 + [ANY] * len(after),
            out_specs=VMEM,
            compiler_params=PARAMS,
            name="merge",
        )(first, second, *after)

    def inner(subs, order, *halos):
        return pl.pallas_call(
            functools.partial(later_kernel, subs),
            out_shape=(
                shape((len(subs), q, full), f32),
                shape((len(subs), 80, half + full), jnp.bfloat16),
                shape((len(subs), q + 32, full), f32),
            ),
            in_specs=[ANY] + [VMEM] * (5 + len(halos) + row_blocks),
            out_specs=(VMEM,) * 3,
            scratch_shapes=[operand],
            compiler_params=PARAMS,
            name="inner_last" if halos else "inner_middle",
        )(order, *fields, *halos, *factor)

    inner_middle, basis_middle, whole_middle = inner(tuple(range(1, count - 1)), own_sums)
    block = pl.pallas_call(
        functools.partial(cross_kernel, copies, share, ranks),
        out_shape=shape((own_rows, copies * cases), f32),
        in_specs=[VMEM] * 3 + [ANY],
        out_specs=VMEM,
        compiler_params=PARAMS,
        name="cross",
    )(own_sums, face_modes, from_before, whole_middle)

    turn = 0
    distance = devices // 2
    while distance >= 1:
        turn += 1
        after = ()
        if turn == 1:
            inner_first, basis_first, right_first, *returned = pl.pallas_call(
                start_kernel,
                out_shape=(
                    shape((1, q, full), f32),
                    shape((1, 80, half + full), jnp.bfloat16),
                    shape((q + 32, half), f32),
                    shape((cut, half), f32),
                    shape((q + 40 - cut, half), f32),
                ),
                in_specs=[ANY] + [VMEM] * (6 + row_blocks),
                out_specs=(VMEM,) * 5,
                scratch_shapes=[operand],
                compiler_params=PARAMS,
                name="inner_first",
            )(block, *fields, from_before, *factor)
            after = (returned[0],)
            received = [shifted(part, -1) for part in returned]
        elif turn == 5:
            inner_last, basis_last, whole_last = inner((count - 1,), block, from_next)
            after = (whole_last,)
        partner = swapped(block, distance)
        if distance >= share:
            block = merged(add_kernel, block.shape, block, partner, *after)
        else:
            if block.ndim == 2:
                block, partner = block[None], partner[None]
            pair = functools.partial(pair_kernel, distance)
            size = block.shape[0]
            block = merged(pair, (size, 2) + block.shape[1:], block, partner, *after)
            block = block.reshape((2 * size,) + block.shape[2:])
        distance //= 2

    projected, coeffs, sums = pl.pallas_call(
        functools.partial(combine_kernel, copies),
        out_shape=(
            shape((count, cases, half), f32),
            shape((8 * (count + 3), cases), f32),
            shape((8, 4 * cases), f32),
        ),
        in_specs=[VMEM] * 11,
        out_specs=(VMEM,) * 3,
        compiler_params=PARAMS,
        name="combine",
    )(
        block,
        from_before,
        coarse_rows,
        from_next,
        masked,
        inner_first,
        basis_first,
        inner_middle,
        basis_middle,
        inner_last,
        basis_last,
    )

    image_proj, image_old = pl.pallas_call(
        outer_kernel,
        out_shape=(shape((count, cases, half), f32),) * 2,
        in_specs=[ANY] + [VMEM] * (5 + row_blocks),
        out_specs=(VMEM,) * 2,
        compiler_params=PARAMS,
        name="outer",
    )(sums, match_copy, whole_middle, whole_last, right_first, coeffs, *factor)
    after = (image_proj,)
    distance = devices // 2
    while distance >= 1:
        sums = merged(add_kernel, sums.shape, sums, swapped(sums, distance), *after)
        after = ()
        distance //= 2

    return pl.pallas_call(
        finish_kernel,
        out_shape=(shape((count, cases, half), f32),) * 3,
        in_specs=[VMEM] * 11,
        out_specs=(VMEM,) * 3,
        compiler_params=PARAMS,
        name="finish",
    )(
        sums,
        old_norms.reshape(1, cases),
        multipliers,
        masked,
        old_masked,
        projected,
        image_proj,
        image_old,
        coeffs,
        *received,
    )


def solution(mesh):
    placed = (
        P(AXES, None, None),
        P(AXES, None, None),
        P(AXES, None, None),
        P(),
        P(AXES, None),
        P(AXES, None, None),
        P(AXES, None, None),
        P(AXES, None),
    )
    return jax.shard_map(
        on_device,
        mesh=mesh,
        in_specs=placed,
        out_specs=(P(AXES, None, None),) * 3,
        check_vma=False,
    )
```

```python
import functools

import jax
import jax.numpy as jnp
from jax import lax
from jax.experimental import pallas as pl
from jax.experimental.pallas import tpu as pltpu
from jax.sharding import PartitionSpec as P

AXES = ("sub", "grp")
HIGHEST = lax.Precision.HIGHEST
VMEM = pl.BlockSpec(memory_space=pltpu.VMEM)
HBM = pl.BlockSpec(memory_space=pltpu.HBM)
BLOCK = 256
ANY = pl.BlockSpec(memory_space=pl.ANY)
PARAMS = pltpu.CompilerParams(vmem_limit_bytes=8 << 20)


def shifted(block, distance):
    devices = range(lax.axis_size(AXES))
    route = [(i - distance, i) for i in devices if i - distance in devices]
    return lax.ppermute(block, AXES, route)


def swapped(block, distance):
    route = [(i, i ^ distance) for i in range(lax.axis_size(AXES))]
    return lax.ppermute(block, AXES, route)


def rows_dot(first, second, precision=None):
    return lax.dot_general(
        first,
        second,
        (((1,), (1,)), ((), ())),
        precision=precision,
        preferred_element_type=jnp.float32,
    )


def plain_dot(first, second, precision=None):
    return lax.dot_general(
        first,
        second,
        (((1,), (0,)), ((), ())),
        precision=precision,
        preferred_element_type=jnp.float32,
    )


def halves(values):
    high = values.astype(jnp.bfloat16)
    low = (values - high.astype(jnp.float32)).astype(jnp.bfloat16)
    return high, low


def thirds(values):
    high = values.astype(jnp.bfloat16)
    rest = values - high.astype(jnp.float32)
    middle = rest.astype(jnp.bfloat16)
    low = (rest - middle.astype(jnp.float32)).astype(jnp.bfloat16)
    return high, middle, low


def match_table(row):
    width = row.shape[1]
    positions = lax.broadcasted_iota(jnp.int32, (width, width), 0)
    return (positions == row).astype(jnp.float32).astype(jnp.bfloat16)


def in_lane_block(values, lane_block, copies):
    cases = values.shape[1]
    wide = jnp.concatenate([values] * copies, axis=1)
    lanes = lax.broadcasted_iota(jnp.int32, wide.shape, 1)
    first = lane_block * cases
    inside = (lanes >= first) & (lanes < first + cases)
    return jnp.where(inside, wide, 0.0)


def first_kernel(modes_in, coarse_in, residual_in, old_in, pack_next, modes, coarse, arrived):
    ranks, count, full = modes_in.shape
    half = full // 2
    width = coarse_in.shape[1]
    pairs = [(modes_in, modes), (coarse_in, coarse)]
    lane = half + width
    for field in (residual_in, old_in):
        for k in range(field.shape[1] // 8):
            pairs.append(
                (field.at[count - 1, pl.ds(8 * k, 8)], pack_next.at[:, pl.ds(lane, half)])
            )
            lane += half
    fetches = [pltpu.make_async_copy(a, b, arrived.at[i]) for i, (a, b) in enumerate(pairs)]
    for fetch in fetches:
        fetch.start()
    pack_next[:, : half + width] = jnp.zeros((8, half + width), jnp.float32)
    fetches[0].wait()
    pack_next[0:ranks, :half] = modes[:, count - 1, half:]
    fetches[1].wait()
    pack_next[0:ranks, half : half + width] = coarse[(count - 1) * ranks : count * ranks, :]
    for fetch in fetches[2:]:
        fetch.wait()


def at_face_before(left, table):
    high, middle, low = thirds(left)
    stacked = jnp.concatenate(
        [high.astype(jnp.float32), middle.astype(jnp.float32), low.astype(jnp.float32), left * 0.0],
        axis=0,
    ).astype(jnp.bfloat16)
    moved = rows_dot(stacked, table)
    return moved[0:8] + moved[8:16] + moved[16:24]


def prepare_kernel(
    copies,
    share,
    matching_in,
    modes_in,
    coarse_in,
    residual_in,
    old_in,
    factor_in,
    face_modes,
    own_sums,
    pack_before,
    masked,
    old_masked,
    padded,
    matching,
    coarse_rows,
    *others,
):
    held, (modes, coarse, arrived) = others[:-3], others[-3:]
    count, cases, half = residual_in.shape
    ranks = modes_in.shape[0]
    fetches = []

    def fetch(source, target):
        copy = pltpu.make_async_copy(source, target, arrived.at[len(fetches)])
        copy.start()
        fetches.append(copy)

    fetch(matching_in, matching)
    fetch(modes_in, modes)
    fetch(residual_in, masked)
    fetch(old_in, old_masked)
    fetch(coarse_in, coarse)
    for a, rows in enumerate(held):
        _, depth, width = rows.shape
        fetch(factor_in.at[:, pl.ds(a * depth, depth), pl.ds(0, width)], rows)
    me = lax.axis_index(AXES)
    keep = jnp.where(me == lax.axis_size(AXES) - 1, 0.0, 1.0)
    lane_block = me // share
    padded[...] = jnp.zeros_like(padded)
    coarse_rows[...] = jnp.zeros_like(coarse_rows)
    fetches[0].wait()
    fetches[1].wait()
    for g in range(count):
        padded[g, 0:ranks, :] = modes[:, g, :]
    for g in range(count):
        face_modes[g] = at_face_before(padded[g, :, :half], match_table(matching[g : g + 1, :]))
    fetches[2].wait()
    masked[count - 1] = masked[count - 1] * keep
    sums = [0.0] * count
    for g in range(count):
        if g == count - 1:
            sums[g] = sums[g] + rows_dot(padded[g, :, half:], masked[g], HIGHEST)
        else:
            both = jnp.concatenate([padded[g, :, half:], face_modes[g + 1]], axis=0)
            found = rows_dot(both, masked[g], HIGHEST)
            sums[g] = sums[g] + found[0:8]
            sums[g + 1] = -found[8:16]
    own_sums[...] = jnp.zeros_like(own_sums)
    for g in range(count):
        own_sums[g * ranks : (g + 1) * ranks, :] = in_lane_block(sums[g], lane_block, copies)[0:ranks]
    fetches[4].wait()
    for g in range(count):
        coarse_rows[8 * g : 8 * g + ranks, :] = coarse[g * ranks : (g + 1) * ranks, :]
    width = half + coarse_rows.shape[1]
    pack_before[:, :half] = face_modes[0]
    pack_before[:, half:width] = coarse_rows[0:8, :]
    pack_before[:, width : width + coarse_rows.shape[1]] = coarse_rows[8:16, :]
    pack_before[:, width + coarse_rows.shape[1] :] = jnp.zeros((8, half), jnp.float32)
    fetches[3].wait()
    old_masked[count - 1] = old_masked[count - 1] * keep
    for copy in fetches[5:]:
        copy.wait()


def cross_kernel(copies, share, ranks, own_sums, face_modes, from_before, order, out):
    lane_block = lax.axis_index(AXES) // share
    half = face_modes.shape[2]
    fields = from_before.shape[1] - 2 * half * (out.shape[1] // copies // 8)
    field = unpacked(from_before, fields, out.shape[1] // copies, half)
    cross = rows_dot(face_modes[0], field, HIGHEST)
    out[...] = own_sums[...]
    out[0:ranks, :] = own_sums[0:ranks, :] - in_lane_block(cross, lane_block, copies)[0:ranks]


def unpacked(pack, start, cases, half):
    return jnp.concatenate(
        [pack[:, start + k * half : start + (k + 1) * half] for k in range(cases // 8)], axis=0
    )


def inner_part(g, matching, padded, masked, old_masked, face_modes, held, from_before, from_next, operand):
    count, cases, half = masked.shape
    full = 2 * half
    block = full // len(held)
    rows = operand.shape[0] // 2
    me = lax.axis_index(AXES)
    q = 2 * cases
    zeros8 = jnp.zeros((8, half), jnp.float32)
    left_modes = padded[g, :, :half]
    right_modes = padded[g, :, half:]
    if g == 0:
        fields = from_before.shape[1] - 2 * half * (cases // 8)
        prior_modes = from_before[:, :half]
        prior_res = unpacked(from_before, fields, cases, half)
        prior_old = unpacked(from_before, fields + half * (cases // 8), cases, half)
        left_modes = left_modes * jnp.where(me == 0, 0.0, 1.0)
    else:
        prior_modes = padded[g - 1, :, half:]
        prior_res, prior_old = masked[g - 1], old_masked[g - 1]
    if g == count - 1:
        keep = jnp.where(me == lax.axis_size(AXES) - 1, 0.0, 1.0)
        next_faces = from_next[:, :half] * keep
        right_modes = right_modes * keep
    else:
        next_faces = face_modes[g + 1]

    right = jnp.concatenate(
        [masked[g], old_masked[g], zeros8, right_modes, -next_faces, zeros8], axis=0
    )
    right_high, right_low = halves(right)
    operand[0:rows, half:] = right_high
    operand[rows:, half:] = right_low

    moving = jnp.concatenate([prior_res, prior_old, prior_modes, zeros8], axis=0)
    high, low = halves(-moving)
    moved = plain_dot(jnp.concatenate([high, low], axis=0), match_table(matching[g : g + 1, :]))
    part = moving.shape[0]
    own_high, own_low = halves(left_modes)
    own_high = own_high.astype(jnp.float32)
    own_low = own_low.astype(jnp.float32)
    operand[0:rows, :half] = jnp.concatenate(
        [moved[0 : q + 8], own_high, zeros8, zeros8], axis=0
    ).astype(jnp.bfloat16)
    operand[rows:, :half] = jnp.concatenate(
        [moved[part : part + q + 8], own_low, zeros8, zeros8], axis=0
    ).astype(jnp.bfloat16)

    pieces = []
    for a in range(len(held)):
        found = rows_dot(operand[:, : (a + 1) * block], held[a][g])
        pieces.append(found[0:rows] + found[rows:])
    return right, jnp.concatenate(pieces, axis=1)


def store_inner(slot, right, found, inner, basis):
    cases, half = inner.shape[1] // 2, right.shape[1]
    q = 2 * cases
    inner[slot] = found[0:q]
    wide = jnp.concatenate([right[q : q + 24], found[q : q + 24]], axis=1)
    basis[slot] = three_terms(wide)


def three_terms(wide):
    high, low = halves(wide)
    high = high.astype(jnp.float32)
    return jnp.concatenate(
        [high, low.astype(jnp.float32), high, jnp.zeros_like(wide[0:8])], axis=0
    ).astype(jnp.bfloat16)


def across(coeffs, terms):
    high, low = halves(coeffs)
    high = high.astype(jnp.float32)
    stacked = jnp.concatenate(
        [high, high, low.astype(jnp.float32), jnp.zeros_like(coeffs[0:8])], axis=0
    ).astype(jnp.bfloat16)
    return lax.dot_general(
        stacked, terms, (((0,), (0,)), ((), ())), preferred_element_type=jnp.float32
    )


def outer_part(g, found, matching, held):
    rows, full = found.shape
    half = full // 2
    block = full // len(held)
    high, low = halves(found)
    operand = jnp.concatenate([high, low], axis=0)
    pieces = [0.0] * len(held)
    for a in range(len(held)):
        part = plain_dot(operand[:, a * block : (a + 1) * block], held[a][g])
        part = part[0:rows] + part[rows:]
        for b in range(a + 1):
            pieces[b] = pieces[b] + part[:, b * block : (b + 1) * block]
    per_half = half // block
    left = jnp.concatenate(pieces[:per_half], axis=1)
    right = jnp.concatenate(pieces[per_half:], axis=1)
    high, low = halves(left)
    moved = rows_dot(jnp.concatenate([high, low], axis=0), match_table(matching[g : g + 1, :]))
    return moved[0:rows] + moved[rows:], right


def later_kernel(subs, order, matching, padded, masked, old_masked, face_modes, *others):
    halos = len(subs) == 1
    from_next = others[0] if halos else None
    held, (inner, basis, whole, operand) = others[halos:-4], others[-4:]
    operand[...] = jnp.zeros_like(operand)
    for slot, g in enumerate(subs):
        right, found = inner_part(
            g, matching, padded, masked, old_masked, face_modes, held, None, from_next, operand
        )
        store_inner(slot, right, found, inner, basis)
        whole[slot] = found


def start_kernel(order, matching, padded, masked, old_masked, face_modes, from_before, *others):
    held, (inner, basis, right_first, returned, returned_rest, operand) = others[:-6], others[-6:]
    operand[...] = jnp.zeros_like(operand)
    right, found = inner_part(
        0, matching, padded, masked, old_masked, face_modes, held, from_before, None, operand
    )
    store_inner(0, right, found, inner, basis)
    moved, solved = outer_part(0, found, matching, held)
    right_first[...] = solved
    cut = returned.shape[0]
    returned[...] = moved[0:cut]
    returned_rest[...] = jnp.zeros_like(returned_rest)
    returned_rest[0 : returned_rest.shape[0] - 8] = moved[cut : cut + returned_rest.shape[0] - 8]


def outer_kernel(order, matching, whole_middle, whole_last, right_first, coeffs, *others):
    held, (image_proj, image_old) = others[:-2], others[-2:]
    count, cases, half = image_proj.shape
    q = 2 * cases
    keep = jnp.where(lax.axis_index(AXES) == lax.axis_size(AXES) - 1, 0.0, 1.0)
    following = jnp.zeros((q + 24, half), jnp.float32)
    zeros8 = jnp.zeros((8, half), jnp.float32)
    for g in reversed(range(count)):
        if g:
            found = whole_last[0] if g == count - 1 else whole_middle[g - 1]
            moved, solved = outer_part(g, found, matching, held)
        else:
            solved = right_first[...]
        both = solved[0:q] - following[0:q]
        basis = jnp.concatenate([solved[q : q + 24], zeros8], axis=0) - jnp.concatenate(
            [zeros8, following[q : q + 24]], axis=0
        )
        if g == count - 1:
            both, basis = both * keep, basis * keep
        image_proj[g] = both[0:cases] - across(coeffs[8 * g : 8 * g + 32], three_terms(basis))
        image_old[g] = both[cases:]
        if g:
            following = moved


def add_kernel(offsets, own, *others):
    total = own[...]
    for k in range(len(offsets)):
        total = total + others[k][...]
    others[-1][...] = total


def place_kernel(offsets, distance, own, *others):
    out = others[-1]
    place = (lax.axis_index(AXES) // distance) % out.shape[1]
    out[:, pl.ds(place, 1)] = own[...][:, None]
    for k, offset in enumerate(offsets):
        out[:, pl.ds(place ^ offset, 1)] = others[k][...][:, None]


def combine_kernel(
    copies,
    gathered,
    from_before,
    coarse_rows,
    from_next,
    masked,
    *others,
):
    parts, (projected, coeffs, sums) = others[:-3], others[-3:]
    count, cases, half = masked.shape
    width = coarse_rows.shape[1]
    own = gathered[...].reshape(gathered.shape[0] * gathered.shape[1], copies * cases)
    stacked = jnp.concatenate([own[:, b * cases : (b + 1) * cases] for b in range(copies)], axis=0)
    rows = jnp.concatenate(
        [
            from_before[:, half : half + width],
            coarse_rows[...],
            from_next[:, half : half + width],
            from_next[:, half + width : half + 2 * width],
        ],
        axis=0,
    )
    high, low = halves(rows)
    stacked_high, stacked_low = halves(stacked)
    depth = rows.shape[0]
    wide = plain_dot(
        jnp.concatenate([high.astype(jnp.float32), low.astype(jnp.float32)], axis=0).astype(
            jnp.bfloat16
        ),
        stacked_high,
    )
    near = wide[0:depth] + wide[depth:] + plain_dot(high, stacked_low)
    coeffs[...] = near
    lanes = 128
    totals = [jnp.zeros((cases, lanes), jnp.float32) for _ in range(4)]

    def folded(values):
        out = values[:, :lanes]
        for k in range(1, values.shape[1] // lanes):
            out = out + values[:, k * lanes : (k + 1) * lanes]
        return out

    for g in range(count):
        place = 0 if g == 0 else 4 if g == count - 1 else 2
        slot = g - 1 if place == 2 else 0
        inner = parts[place][slot]
        spread = across(near[8 * g : 8 * g + 24], parts[place + 1][slot])
        proj = masked[g] - spread[:, :half]
        mine = inner[0:cases] - spread[:, half:]
        other = inner[cases:]
        projected[g] = proj
        totals[0] += folded(proj * proj)
        totals[1] += folded(mine * mine)
        totals[2] += folded(mine * other)
        totals[3] += folded(other * other)
    high, low = halves(jnp.concatenate(totals, axis=0))
    ones = jnp.ones((8, lanes), jnp.bfloat16)
    sums[...] = rows_dot(ones, high) + rows_dot(ones, low)


def finish_kernel(
    sums,
    old_norms,
    multipliers,
    masked,
    old_masked,
    projected,
    image_proj,
    image_old,
    coeffs,
    received_first,
    received_rest,
    new_multipliers,
    new_residual,
    direction,
):
    count, cases, half = masked.shape
    diagonal = lax.broadcasted_iota(jnp.int32, (cases, cases), 0) == lax.broadcasted_iota(
        jnp.int32, (cases, cases), 1
    )

    def column(row):
        return jnp.sum(jnp.where(diagonal, row, 0.0), axis=1, keepdims=True)

    norms = sums[0:1, 0:cases]
    ratio = norms / old_norms[...]
    curvature = (
        sums[0:1, cases : 2 * cases]
        + 2.0 * ratio * sums[0:1, 2 * cases : 3 * cases]
        + ratio * ratio * sums[0:1, 3 * cases : 4 * cases]
    )
    step_len = column(norms / curvature)
    ratio = column(ratio)
    for g in range(count):
        image_p, image_o = image_proj[g], image_old[g]
        if g == count - 1:
            received = jnp.concatenate([received_first[...], received_rest[...]], axis=0)
            basis = three_terms(received[2 * cases : 2 * cases + 24])
            near = coeffs[8 * count : 8 * count + 24]
            image_p = image_p - received[0:cases] + across(near, basis)
            image_o = image_o - received[cases : 2 * cases]
        towards = projected[g] + ratio * old_masked[g]
        direction[g] = towards
        new_multipliers[g] = multipliers[g] + step_len * towards
        new_residual[g] = masked[g] - step_len * (image_p + ratio * image_o)


def on_device(
    multipliers,
    residual,
    old_direction,
    old_norms,
    matching,
    factor_inverse,
    rigid_modes,
    coarse_inverse,
):
    count, cases, half = residual.shape
    ranks = rigid_modes.shape[1]
    full = factor_inverse.shape[1]
    own_rows, coarse_width = coarse_inverse.shape
    devices = lax.axis_size(AXES)
    copies = min(128 // cases, devices)
    share = devices // copies
    f32 = jnp.float32
    shape = jax.ShapeDtypeStruct
    row_block = min(BLOCK, full)
    row_blocks = full // row_block
    q = 2 * cases
    cut = q - 8
    in_hbm = lambda *arrays: (pltpu.with_memory_space_constraint(x, pltpu.HBM) for x in arrays)

    modes_by_rank = rigid_modes.transpose(1, 0, 2)
    next_width = half + coarse_width + 2 * half * (cases // 8)
    pack_next = pl.pallas_call(
        first_kernel,
        out_shape=shape((8, next_width), f32),
        in_specs=[HBM] * 4,
        out_specs=VMEM,
        scratch_shapes=[
            pltpu.VMEM((ranks, count, full), f32),
            pltpu.VMEM((own_rows, coarse_width), f32),
            pltpu.SemaphoreType.DMA((2 + 2 * (cases // 8),)),
        ],
        compiler_params=PARAMS,
        name="first",
    )(*in_hbm(modes_by_rank, coarse_inverse, residual, old_direction))

    from_before = shifted(pack_next, 1)

    (
        face_modes,
        own_sums,
        pack_before,
        masked,
        old_masked,
        padded,
        match_copy,
        coarse_rows,
        *factor,
    ) = pl.pallas_call(
        functools.partial(prepare_kernel, copies, share),
        out_shape=(
            shape((count, 8, half), f32),
            shape((own_rows, copies * cases), f32),
            shape((8, 2 * half + 2 * coarse_width), f32),
            shape((count, cases, half), f32),
            shape((count, cases, half), f32),
            shape((count, 8, full), f32),
            shape((count, half), jnp.int32),
            shape((8 * count, coarse_width), f32),
        )
        + tuple(
            shape((count, row_block, (a + 1) * row_block), jnp.bfloat16) for a in range(row_blocks)
        ),
        in_specs=[HBM] * 6,
        out_specs=(VMEM,) * (8 + row_blocks),
        scratch_shapes=[
            pltpu.VMEM((ranks, count, full), f32),
            pltpu.VMEM((own_rows, coarse_width), f32),
            pltpu.SemaphoreType.DMA((5 + row_blocks,)),
        ],
        compiler_params=PARAMS,
        name="prepare",
    )(
        *in_hbm(
            matching, modes_by_rank, coarse_inverse, residual, old_direction, factor_inverse
        )
    )

    from_next = shifted(pack_before, -1)

    operand = pltpu.VMEM((2 * (q + 32), full), jnp.bfloat16)
    fields = (match_copy, padded, masked, old_masked, face_modes)

    def exchanged(block, distance, width, placed, *after):
        offsets = tuple(range(1, width))
        partners = [swapped(block, k * distance) for k in offsets]
        size = block.shape
        if placed:
            kernel = functools.partial(place_kernel, offsets, distance)
            size = (block.shape[0], width) + block.shape[1:]
        else:
            kernel = functools.partial(add_kernel, offsets)
        return pl.pallas_call(
            kernel,
            out_shape=shape(size, f32),
            in_specs=[VMEM] * width + [ANY] * len(after),
            out_specs=VMEM,
            compiler_params=PARAMS,
            name="merge",
        )(block, *partners, *after)

    def rounds_of(most):
        rounds = []
        distance = devices
        while distance > 1:
            width = most if 2 * most <= distance <= share else 2
            distance //= width
            rounds.append((distance, width))
        return rounds

    rounds = rounds_of(2)

    def inner(subs, order, *halos):
        return pl.pallas_call(
            functools.partial(later_kernel, subs),
            out_shape=(
                shape((len(subs), q, full), f32),
                shape((len(subs), 80, half + full), jnp.bfloat16),
                shape((len(subs), q + 32, full), f32),
            ),
            in_specs=[ANY] + [VMEM] * (5 + len(halos) + row_blocks),
            out_specs=(VMEM,) * 3,
            scratch_shapes=[operand],
            compiler_params=PARAMS,
            name="inner_last" if halos else "inner_middle",
        )(order, *fields, *halos, *factor)

    inner_middle, basis_middle, whole_middle = inner(tuple(range(1, count - 1)), own_sums)
    block = pl.pallas_call(
        functools.partial(cross_kernel, copies, share, ranks),
        out_shape=shape((own_rows, copies * cases), f32),
        in_specs=[VMEM] * 3 + [ANY],
        out_specs=VMEM,
        compiler_params=PARAMS,
        name="cross",
    )(own_sums, face_modes, from_before, whole_middle)

    for turn, (distance, width) in enumerate(rounds):
        after = ()
        if turn == 0:
            inner_first, basis_first, right_first, *returned = pl.pallas_call(
                start_kernel,
                out_shape=(
                    shape((1, q, full), f32),
                    shape((1, 80, half + full), jnp.bfloat16),
                    shape((q + 32, half), f32),
                    shape((cut, half), f32),
                    shape((q + 24 + 8 - cut, half), f32),
                ),
                in_specs=[ANY] + [VMEM] * (6 + row_blocks),
                out_specs=(VMEM,) * 5,
                scratch_shapes=[operand],
                compiler_params=PARAMS,
                name="inner_first",
            )(block, *fields, from_before, *factor)
            after = (returned[0],)
            received = [shifted(part, -1) for part in returned]
        elif turn == len(rounds) - 1:
            inner_last, basis_last, whole_last = inner((count - 1,), block, from_next)
            after = (whole_last,)
        placed = distance < share
        if placed and block.ndim == 2:
            block = block[None]
        block = exchanged(block, distance, width, placed, *after)
        if placed:
            block = block.reshape((-1,) + block.shape[2:])

    projected, coeffs, sums = pl.pallas_call(
        functools.partial(combine_kernel, copies),
        out_shape=(
            shape((count, cases, half), f32),
            shape((8 * (count + 3), cases), f32),
            shape((8, 4 * cases), f32),
        ),
        in_specs=[VMEM] * 11,
        out_specs=(VMEM,) * 3,
        compiler_params=PARAMS,
        name="combine",
    )(
        block,
        from_before,
        coarse_rows,
        from_next,
        masked,
        inner_first,
        basis_first,
        inner_middle,
        basis_middle,
        inner_last,
        basis_last,
    )

    image_proj, image_old = pl.pallas_call(
        outer_kernel,
        out_shape=(shape((count, cases, half), f32),) * 2,
        in_specs=[ANY] + [VMEM] * (5 + row_blocks),
        out_specs=(VMEM,) * 2,
        compiler_params=PARAMS,
        name="outer",
    )(sums, match_copy, whole_middle, whole_last, right_first, coeffs, *factor)
    after = (image_proj,)
    for distance, width in rounds_of(4):
        sums = exchanged(sums, distance, width, False, *after)
        after = ()

    return pl.pallas_call(
        finish_kernel,
        out_shape=(shape((count, cases, half), f32),) * 3,
        in_specs=[VMEM] * 11,
        out_specs=(VMEM,) * 3,
        compiler_params=PARAMS,
        name="finish",
    )(
        sums,
        old_norms.reshape(1, cases),
        multipliers,
        masked,
        old_masked,
        projected,
        image_proj,
        image_old,
        coeffs,
        *received,
    )


def solution(mesh):
    placed = (
        P(AXES, None, None),
        P(AXES, None, None),
        P(AXES, None, None),
        P(),
        P(AXES, None),
        P(AXES, None, None),
        P(AXES, None, None),
        P(AXES, None),
    )
    return jax.shard_map(
        on_device,
        mesh=mesh,
        in_specs=placed,
        out_specs=(P(AXES, None, None),) * 3,
        check_vma=False,
    )
```

```python
import functools

import jax
import jax.numpy as jnp
from jax import lax
from jax.experimental import pallas as pl
from jax.experimental.pallas import tpu as pltpu
from jax.sharding import PartitionSpec as P

AXES = ("sub", "grp")
HIGHEST = lax.Precision.HIGHEST
VMEM = pl.BlockSpec(memory_space=pltpu.VMEM)
HBM = pl.BlockSpec(memory_space=pltpu.HBM)
BLOCK = 256
ANY = pl.BlockSpec(memory_space=pl.ANY)
PARAMS = pltpu.CompilerParams(vmem_limit_bytes=8 << 20)


def shifted(block, distance):
    devices = range(lax.axis_size(AXES))
    route = [(i - distance, i) for i in devices if i - distance in devices]
    return lax.ppermute(block, AXES, route)


def swapped(block, distance):
    route = [(i, i ^ distance) for i in range(lax.axis_size(AXES))]
    return lax.ppermute(block, AXES, route)


def rows_dot(first, second, precision=None):
    return lax.dot_general(
        first,
        second,
        (((1,), (1,)), ((), ())),
        precision=precision,
        preferred_element_type=jnp.float32,
    )


def plain_dot(first, second, precision=None):
    return lax.dot_general(
        first,
        second,
        (((1,), (0,)), ((), ())),
        precision=precision,
        preferred_element_type=jnp.float32,
    )


def halves(values):
    high = values.astype(jnp.bfloat16)
    low = (values - high.astype(jnp.float32)).astype(jnp.bfloat16)
    return high, low


def thirds(values):
    high = values.astype(jnp.bfloat16)
    rest = values - high.astype(jnp.float32)
    middle = rest.astype(jnp.bfloat16)
    low = (rest - middle.astype(jnp.float32)).astype(jnp.bfloat16)
    return high, middle, low


def match_table(row):
    width = row.shape[1]
    positions = lax.broadcasted_iota(jnp.int32, (width, width), 0)
    return (positions == row).astype(jnp.float32).astype(jnp.bfloat16)


def in_lane_block(values, lane_block, copies):
    cases = values.shape[1]
    wide = jnp.concatenate([values] * copies, axis=1)
    lanes = lax.broadcasted_iota(jnp.int32, wide.shape, 1)
    first = lane_block * cases
    inside = (lanes >= first) & (lanes < first + cases)
    return jnp.where(inside, wide, 0.0)


def first_kernel(modes_in, coarse_in, residual_in, old_in, pack_next, modes, coarse, arrived):
    ranks, count, full = modes_in.shape
    _, cases, half = residual_in.shape
    rows, width = coarse.shape
    last = count - 1
    pairs = [
        (modes_in.at[:, :, pl.ds(half, half)], modes),
        (coarse_in.at[pl.ds(coarse_in.shape[0] - rows, rows)], coarse),
        (residual_in.at[last], pack_next.at[pl.ds(0, cases)]),
        (old_in.at[last], pack_next.at[pl.ds(cases, cases)]),
    ]
    fetches = [pltpu.make_async_copy(a, b, arrived.at[i]) for i, (a, b) in enumerate(pairs)]
    for fetch in fetches:
        fetch.start()
    row = 2 * cases
    pack_next[row:, :] = jnp.zeros((pack_next.shape[0] - row, half), jnp.float32)
    fetches[0].wait()
    pack_next[row : row + ranks, :] = modes[:, last, :]
    fetches[1].wait()
    for lane in range(0, width, half):
        row += 8
        part = coarse[rows - ranks :, lane : min(lane + half, width)]
        pack_next[row : row + ranks, : part.shape[1]] = part
    fetches[2].wait()
    fetches[3].wait()


def at_face_before(left, table):
    high, middle, low = thirds(left)
    stacked = jnp.concatenate(
        [high.astype(jnp.float32), middle.astype(jnp.float32), low.astype(jnp.float32), left * 0.0],
        axis=0,
    ).astype(jnp.bfloat16)
    moved = rows_dot(stacked, table)
    return moved[0:8] + moved[8:16] + moved[16:24]


def prepare_kernel(
    copies,
    share,
    matching_in,
    modes_in,
    coarse_in,
    residual_in,
    old_in,
    factor_in,
    face_modes,
    own_sums,
    pack_before,
    masked,
    old_masked,
    padded,
    matching,
    coarse_rows,
    *others,
):
    held, (modes, coarse, arrived) = others[:-3], others[-3:]
    count, cases, half = residual_in.shape
    ranks = modes_in.shape[0]
    fetches = []

    def fetch(source, target):
        copy = pltpu.make_async_copy(source, target, arrived.at[len(fetches)])
        copy.start()
        fetches.append(copy)

    fetch(matching_in, matching)
    fetch(modes_in, modes)
    fetch(residual_in, masked)
    fetch(old_in, old_masked)
    fetch(coarse_in, coarse)
    for a, rows in enumerate(held):
        _, depth, width = rows.shape
        fetch(factor_in.at[:, pl.ds(a * depth, depth), pl.ds(0, width)], rows)
    me = lax.axis_index(AXES)
    keep = jnp.where(me == lax.axis_size(AXES) - 1, 0.0, 1.0)
    lane_block = me // share
    padded[...] = jnp.zeros_like(padded)
    coarse_rows[...] = jnp.zeros_like(coarse_rows)
    fetches[0].wait()
    fetches[1].wait()
    for g in range(count):
        padded[g, 0:ranks, :] = modes[:, g, :]
    for g in range(count):
        face_modes[g] = at_face_before(padded[g, :, :half], match_table(matching[g : g + 1, :]))
    fetches[2].wait()
    masked[count - 1] = masked[count - 1] * keep
    sums = [0.0] * count
    for g in range(count):
        if g == count - 1:
            sums[g] = sums[g] + rows_dot(padded[g, :, half:], masked[g], HIGHEST)
        else:
            both = jnp.concatenate([padded[g, :, half:], face_modes[g + 1]], axis=0)
            found = rows_dot(both, masked[g], HIGHEST)
            sums[g] = sums[g] + found[0:8]
            sums[g + 1] = -found[8:16]
    own_sums[...] = jnp.zeros_like(own_sums)
    for g in range(count):
        own_sums[g * ranks : (g + 1) * ranks, :] = in_lane_block(sums[g], lane_block, copies)[0:ranks]
    fetches[4].wait()
    for g in range(count):
        coarse_rows[8 * g : 8 * g + ranks, :] = coarse[g * ranks : (g + 1) * ranks, :]
    width = half + coarse_rows.shape[1]
    pack_before[:, :half] = face_modes[0]
    pack_before[:, half:width] = coarse_rows[0:8, :]
    pack_before[:, width : width + coarse_rows.shape[1]] = coarse_rows[8:16, :]
    pack_before[:, width + coarse_rows.shape[1] :] = jnp.zeros((8, half), jnp.float32)
    fetches[3].wait()
    old_masked[count - 1] = old_masked[count - 1] * keep
    for copy in fetches[5:]:
        copy.wait()


def cross_kernel(copies, share, ranks, own_sums, face_modes, from_before, order, out):
    lane_block = lax.axis_index(AXES) // share
    cases = out.shape[1] // copies
    cross = rows_dot(face_modes[0], from_before[0:cases], HIGHEST)
    out[...] = own_sums[...]
    out[0:ranks, :] = own_sums[0:ranks, :] - in_lane_block(cross, lane_block, copies)[0:ranks]


def inner_part(g, matching, padded, masked, old_masked, face_modes, held, from_before, from_next, operand):
    count, cases, half = masked.shape
    full = 2 * half
    block = full // len(held)
    rows = operand.shape[0] // 2
    me = lax.axis_index(AXES)
    q = 2 * cases
    zeros8 = jnp.zeros((8, half), jnp.float32)
    left_modes = padded[g, :, :half]
    right_modes = padded[g, :, half:]
    if g == 0:
        prior_res, prior_old = from_before[0:cases], from_before[cases : 2 * cases]
        prior_modes = from_before[2 * cases : 2 * cases + 8]
        left_modes = left_modes * jnp.where(me == 0, 0.0, 1.0)
    else:
        prior_modes = padded[g - 1, :, half:]
        prior_res, prior_old = masked[g - 1], old_masked[g - 1]
    if g == count - 1:
        keep = jnp.where(me == lax.axis_size(AXES) - 1, 0.0, 1.0)
        next_faces = from_next[:, :half] * keep
        right_modes = right_modes * keep
    else:
        next_faces = face_modes[g + 1]

    right = jnp.concatenate(
        [masked[g], old_masked[g], zeros8, right_modes, -next_faces, zeros8], axis=0
    )
    right_high, right_low = halves(right)
    operand[0:rows, half:] = right_high
    operand[rows:, half:] = right_low

    moving = jnp.concatenate([prior_res, prior_old, prior_modes, zeros8], axis=0)
    high, low = halves(-moving)
    moved = plain_dot(jnp.concatenate([high, low], axis=0), match_table(matching[g : g + 1, :]))
    part = moving.shape[0]
    own_high, own_low = halves(left_modes)
    own_high = own_high.astype(jnp.float32)
    own_low = own_low.astype(jnp.float32)
    operand[0:rows, :half] = jnp.concatenate(
        [moved[0 : q + 8], own_high, zeros8, zeros8], axis=0
    ).astype(jnp.bfloat16)
    operand[rows:, :half] = jnp.concatenate(
        [moved[part : part + q + 8], own_low, zeros8, zeros8], axis=0
    ).astype(jnp.bfloat16)

    pieces = []
    for a in range(len(held)):
        found = rows_dot(operand[:, : (a + 1) * block], held[a][g])
        pieces.append(found[0:rows] + found[rows:])
    return right, jnp.concatenate(pieces, axis=1)


def store_inner(slot, right, found, inner, basis):
    cases, half = inner.shape[1] // 2, right.shape[1]
    q = 2 * cases
    inner[slot] = found[0:q]
    wide = jnp.concatenate([right[q : q + 24], found[q : q + 24]], axis=1)
    basis[slot] = three_terms(wide)


def three_terms(wide):
    high, low = halves(wide)
    high = high.astype(jnp.float32)
    return jnp.concatenate(
        [high, low.astype(jnp.float32), high, jnp.zeros_like(wide[0:8])], axis=0
    ).astype(jnp.bfloat16)


def across(coeffs, terms):
    high, low = halves(coeffs)
    high = high.astype(jnp.float32)
    stacked = jnp.concatenate(
        [high, high, low.astype(jnp.float32), jnp.zeros_like(coeffs[0:8])], axis=0
    ).astype(jnp.bfloat16)
    return lax.dot_general(
        stacked, terms, (((0,), (0,)), ((), ())), preferred_element_type=jnp.float32
    )


def outer_part(g, found, matching, held):
    rows, full = found.shape
    half = full // 2
    block = full // len(held)
    high, low = halves(found)
    operand = jnp.concatenate([high, low], axis=0)
    pieces = [0.0] * len(held)
    for a in range(len(held)):
        part = plain_dot(operand[:, a * block : (a + 1) * block], held[a][g])
        part = part[0:rows] + part[rows:]
        for b in range(a + 1):
            pieces[b] = pieces[b] + part[:, b * block : (b + 1) * block]
    per_half = half // block
    left = jnp.concatenate(pieces[:per_half], axis=1)
    right = jnp.concatenate(pieces[per_half:], axis=1)
    high, low = halves(left)
    moved = rows_dot(jnp.concatenate([high, low], axis=0), match_table(matching[g : g + 1, :]))
    return moved[0:rows] + moved[rows:], right


def later_kernel(subs, order, matching, padded, masked, old_masked, face_modes, *others):
    halos = len(subs) == 1
    from_next = others[0] if halos else None
    held, (inner, basis, whole, operand) = others[halos:-4], others[-4:]
    operand[...] = jnp.zeros_like(operand)
    for slot, g in enumerate(subs):
        right, found = inner_part(
            g, matching, padded, masked, old_masked, face_modes, held, None, from_next, operand
        )
        store_inner(slot, right, found, inner, basis)
        whole[slot] = found


def start_kernel(order, matching, padded, masked, old_masked, face_modes, from_before, *others):
    held, (inner, basis, right_first, returned, returned_rest, operand) = others[:-6], others[-6:]
    operand[...] = jnp.zeros_like(operand)
    right, found = inner_part(
        0, matching, padded, masked, old_masked, face_modes, held, from_before, None, operand
    )
    store_inner(0, right, found, inner, basis)
    moved, solved = outer_part(0, found, matching, held)
    right_first[...] = solved
    cut = returned.shape[0]
    returned[...] = moved[0:cut]
    returned_rest[...] = jnp.zeros_like(returned_rest)
    returned_rest[0 : returned_rest.shape[0] - 8] = moved[cut : cut + returned_rest.shape[0] - 8]


def outer_kernel(order, matching, whole_middle, whole_last, right_first, coeffs, *others):
    held, (image_proj, image_old) = others[:-2], others[-2:]
    count, cases, half = image_proj.shape
    q = 2 * cases
    keep = jnp.where(lax.axis_index(AXES) == lax.axis_size(AXES) - 1, 0.0, 1.0)
    following = jnp.zeros((q + 24, half), jnp.float32)
    zeros8 = jnp.zeros((8, half), jnp.float32)
    for g in reversed(range(count)):
        if g:
            found = whole_last[0] if g == count - 1 else whole_middle[g - 1]
            moved, solved = outer_part(g, found, matching, held)
        else:
            solved = right_first[...]
        both = solved[0:q] - following[0:q]
        basis = jnp.concatenate([solved[q : q + 24], zeros8], axis=0) - jnp.concatenate(
            [zeros8, following[q : q + 24]], axis=0
        )
        if g == count - 1:
            both, basis = both * keep, basis * keep
        image_proj[g] = both[0:cases] - across(coeffs[8 * g : 8 * g + 32], three_terms(basis))
        image_old[g] = both[cases:]
        if g:
            following = moved


def add_kernel(offsets, own, *others):
    total = own[...]
    for k in range(len(offsets)):
        total = total + others[k][...]
    others[-1][...] = total


def place_kernel(offsets, distance, own, *others):
    out = others[-1]
    place = (lax.axis_index(AXES) // distance) % out.shape[1]
    out[:, pl.ds(place, 1)] = own[...][:, None]
    for k, offset in enumerate(offsets):
        out[:, pl.ds(place ^ offset, 1)] = others[k][...][:, None]


def combine_kernel(
    copies,
    gathered,
    from_before,
    coarse_rows,
    from_next,
    masked,
    *others,
):
    parts, (projected, coeffs, sums) = others[:-3], others[-3:]
    count, cases, half = masked.shape
    width = coarse_rows.shape[1]
    own = gathered[...].reshape(gathered.shape[0] * gathered.shape[1], copies * cases)
    stacked = jnp.concatenate([own[:, b * cases : (b + 1) * cases] for b in range(copies)], axis=0)
    first = 2 * cases + 8
    prior = jnp.concatenate(
        [from_before[k : k + 8] for k in range(first, from_before.shape[0], 8)], axis=1
    )
    rows = jnp.concatenate(
        [
            prior[:, :width],
            coarse_rows[...],
            from_next[:, half : half + width],
            from_next[:, half + width : half + 2 * width],
        ],
        axis=0,
    )
    high, low = halves(rows)
    stacked_high, stacked_low = halves(stacked)
    depth = rows.shape[0]
    wide = plain_dot(
        jnp.concatenate([high.astype(jnp.float32), low.astype(jnp.float32)], axis=0).astype(
            jnp.bfloat16
        ),
        stacked_high,
    )
    near = wide[0:depth] + wide[depth:] + plain_dot(high, stacked_low)
    coeffs[...] = near
    lanes = 128
    totals = [jnp.zeros((cases, lanes), jnp.float32) for _ in range(4)]

    def folded(values):
        out = values[:, :lanes]
        for k in range(1, values.shape[1] // lanes):
            out = out + values[:, k * lanes : (k + 1) * lanes]
        return out

    for g in range(count):
        place = 0 if g == 0 else 4 if g == count - 1 else 2
        slot = g - 1 if place == 2 else 0
        inner = parts[place][slot]
        spread = across(near[8 * g : 8 * g + 24], parts[place + 1][slot])
        proj = masked[g] - spread[:, :half]
        mine = inner[0:cases] - spread[:, half:]
        other = inner[cases:]
        projected[g] = proj
        totals[0] += folded(proj * proj)
        totals[1] += folded(mine * mine)
        totals[2] += folded(mine * other)
        totals[3] += folded(other * other)
    high, low = halves(jnp.concatenate(totals, axis=0))
    ones = jnp.ones((8, lanes), jnp.bfloat16)
    sums[...] = rows_dot(ones, high) + rows_dot(ones, low)


def settle_kernel(order, image_proj, image_old, coeffs, received_first, received_rest, proj, old):
    count, cases, _ = image_proj.shape
    received = jnp.concatenate([received_first[...], received_rest[...]], axis=0)
    basis = three_terms(received[2 * cases : 2 * cases + 24])
    near = coeffs[8 * count : 8 * count + 24]
    proj[...] = image_proj[count - 1] - received[0:cases] + across(near, basis)
    old[...] = image_old[count - 1] - received[cases : 2 * cases]


def finish_kernel(
    sums,
    old_norms,
    multipliers,
    masked,
    old_masked,
    projected,
    image_proj,
    image_old,
    last_proj,
    last_old,
    new_multipliers,
    new_residual,
    direction,
):
    count, cases, half = masked.shape
    diagonal = lax.broadcasted_iota(jnp.int32, (cases, cases), 0) == lax.broadcasted_iota(
        jnp.int32, (cases, cases), 1
    )

    def column(row):
        return jnp.sum(jnp.where(diagonal, row, 0.0), axis=1, keepdims=True)

    norms = sums[0:1, 0:cases]
    ratio = norms / old_norms[...]
    curvature = (
        sums[0:1, cases : 2 * cases]
        + 2.0 * ratio * sums[0:1, 2 * cases : 3 * cases]
        + ratio * ratio * sums[0:1, 3 * cases : 4 * cases]
    )
    step_len = column(norms / curvature)
    ratio = column(ratio)
    for g in range(count):
        image_p, image_o = image_proj[g], image_old[g]
        if g == count - 1:
            image_p, image_o = last_proj[...], last_old[...]
        towards = projected[g] + ratio * old_masked[g]
        direction[g] = towards
        new_multipliers[g] = multipliers[g] + step_len * towards
        new_residual[g] = masked[g] - step_len * (image_p + ratio * image_o)


def on_device(
    multipliers,
    residual,
    old_direction,
    old_norms,
    matching,
    factor_inverse,
    rigid_modes,
    coarse_inverse,
):
    count, cases, half = residual.shape
    ranks = rigid_modes.shape[1]
    full = factor_inverse.shape[1]
    own_rows, coarse_width = coarse_inverse.shape
    devices = lax.axis_size(AXES)
    copies = min(128 // cases, devices)
    share = devices // copies
    f32 = jnp.float32
    shape = jax.ShapeDtypeStruct
    row_block = min(BLOCK, full)
    row_blocks = full // row_block
    q = 2 * cases
    cut = q - 8
    in_hbm = lambda *arrays: (pltpu.with_memory_space_constraint(x, pltpu.HBM) for x in arrays)

    modes_by_rank = rigid_modes.transpose(1, 0, 2)
    next_rows = 2 * cases + 8 + 8 * pl.cdiv(coarse_width, half)
    coarse_part = own_rows - (own_rows - ranks) // 8 * 8
    pack_next = pl.pallas_call(
        first_kernel,
        out_shape=shape((next_rows, half), f32),
        in_specs=[HBM] * 4,
        out_specs=VMEM,
        scratch_shapes=[
            pltpu.VMEM((ranks, count, half), f32),
            pltpu.VMEM((coarse_part, coarse_width), f32),
            pltpu.SemaphoreType.DMA((4,)),
        ],
        compiler_params=PARAMS,
        name="first",
    )(*in_hbm(modes_by_rank, coarse_inverse, residual, old_direction))

    from_before = shifted(pack_next, 1)

    (
        face_modes,
        own_sums,
        pack_before,
        masked,
        old_masked,
        padded,
        match_copy,
        coarse_rows,
        *factor,
    ) = pl.pallas_call(
        functools.partial(prepare_kernel, copies, share),
        out_shape=(
            shape((count, 8, half), f32),
            shape((own_rows, copies * cases), f32),
            shape((8, 2 * half + 2 * coarse_width), f32),
            shape((count, cases, half), f32),
            shape((count, cases, half), f32),
            shape((count, 8, full), f32),
            shape((count, half), jnp.int32),
            shape((8 * count, coarse_width), f32),
        )
        + tuple(
            shape((count, row_block, (a + 1) * row_block), jnp.bfloat16) for a in range(row_blocks)
        ),
        in_specs=[HBM] * 6,
        out_specs=(VMEM,) * (8 + row_blocks),
        scratch_shapes=[
            pltpu.VMEM((ranks, count, full), f32),
            pltpu.VMEM((own_rows, coarse_width), f32),
            pltpu.SemaphoreType.DMA((5 + row_blocks,)),
        ],
        compiler_params=PARAMS,
        name="prepare",
    )(
        *in_hbm(
            matching, modes_by_rank, coarse_inverse, residual, old_direction, factor_inverse
        )
    )

    from_next = shifted(pack_before, -1)

    operand = pltpu.VMEM((2 * (q + 32), full), jnp.bfloat16)
    fields = (match_copy, padded, masked, old_masked, face_modes)

    def exchanged(block, distance, width, placed, *after):
        offsets = tuple(range(1, width))
        partners = [swapped(block, k * distance) for k in offsets]
        size = block.shape
        if placed:
            kernel = functools.partial(place_kernel, offsets, distance)
            size = (block.shape[0], width) + block.shape[1:]
        else:
            kernel = functools.partial(add_kernel, offsets)
        return pl.pallas_call(
            kernel,
            out_shape=shape(size, f32),
            in_specs=[VMEM] * width + [ANY] * len(after),
            out_specs=VMEM,
            compiler_params=PARAMS,
            name="merge",
        )(block, *partners, *after)

    def rounds_of(most):
        rounds = []
        distance = devices
        while distance > 1:
            width = most if 2 * most <= distance <= share else 2
            distance //= width
            rounds.append((distance, width))
        return rounds

    rounds = rounds_of(2)

    def inner(subs, order, *halos):
        return pl.pallas_call(
            functools.partial(later_kernel, subs),
            out_shape=(
                shape((len(subs), q, full), f32),
                shape((len(subs), 80, half + full), jnp.bfloat16),
                shape((len(subs), q + 32, full), f32),
            ),
            in_specs=[ANY] + [VMEM] * (5 + len(halos) + row_blocks),
            out_specs=(VMEM,) * 3,
            scratch_shapes=[operand],
            compiler_params=PARAMS,
            name="inner_last" if halos else "inner_middle",
        )(order, *fields, *halos, *factor)

    inner_middle, basis_middle, whole_middle = inner(tuple(range(1, count - 1)), own_sums)
    block = pl.pallas_call(
        functools.partial(cross_kernel, copies, share, ranks),
        out_shape=shape((own_rows, copies * cases), f32),
        in_specs=[VMEM] * 3 + [ANY],
        out_specs=VMEM,
        compiler_params=PARAMS,
        name="cross",
    )(own_sums, face_modes, from_before, whole_middle)

    for turn, (distance, width) in enumerate(rounds):
        after = ()
        if turn == 0:
            inner_first, basis_first, right_first, *returned = pl.pallas_call(
                start_kernel,
                out_shape=(
                    shape((1, q, full), f32),
                    shape((1, 80, half + full), jnp.bfloat16),
                    shape((q + 32, half), f32),
                    shape((cut, half), f32),
                    shape((q + 24 + 8 - cut, half), f32),
                ),
                in_specs=[ANY] + [VMEM] * (6 + row_blocks),
                out_specs=(VMEM,) * 5,
                scratch_shapes=[operand],
                compiler_params=PARAMS,
                name="inner_first",
            )(block, *fields, from_before, *factor)
            after = (returned[0],)
            received = [shifted(part, -1) for part in returned]
        elif turn == len(rounds) - 1:
            inner_last, basis_last, whole_last = inner((count - 1,), block, from_next)
            after = (whole_last,)
        placed = distance < share
        if placed and block.ndim == 2:
            block = block[None]
        block = exchanged(block, distance, width, placed, *after)
        if placed:
            block = block.reshape((-1,) + block.shape[2:])

    projected, coeffs, sums = pl.pallas_call(
        functools.partial(combine_kernel, copies),
        out_shape=(
            shape((count, cases, half), f32),
            shape((8 * (count + 3), cases), f32),
            shape((8, 4 * cases), f32),
        ),
        in_specs=[VMEM] * 11,
        out_specs=(VMEM,) * 3,
        compiler_params=PARAMS,
        name="combine",
    )(
        block,
        from_before,
        coarse_rows,
        from_next,
        masked,
        inner_first,
        basis_first,
        inner_middle,
        basis_middle,
        inner_last,
        basis_last,
    )

    image_proj, image_old = pl.pallas_call(
        outer_kernel,
        out_shape=(shape((count, cases, half), f32),) * 2,
        in_specs=[ANY] + [VMEM] * (5 + row_blocks),
        out_specs=(VMEM,) * 2,
        compiler_params=PARAMS,
        name="outer",
    )(sums, match_copy, whole_middle, whole_last, right_first, coeffs, *factor)
    after = (image_proj,)
    rounds = sorted(rounds_of(4), key=lambda one: -one[1])
    for distance, width in rounds:
        if distance == rounds[-1][0]:
            last_proj, last_old = pl.pallas_call(
                settle_kernel,
                out_shape=(shape((cases, half), f32),) * 2,
                in_specs=[ANY] + [VMEM] * 5,
                out_specs=(VMEM,) * 2,
                compiler_params=PARAMS,
                name="settle",
            )(sums, image_proj, image_old, coeffs, *received)
            after = (last_proj,)
        sums = exchanged(sums, distance, width, False, *after)
        after = ()

    return pl.pallas_call(
        finish_kernel,
        out_shape=(shape((count, cases, half), f32),) * 3,
        in_specs=[VMEM] * 10,
        out_specs=(VMEM,) * 3,
        compiler_params=PARAMS,
        name="finish",
    )(
        sums,
        old_norms.reshape(1, cases),
        multipliers,
        masked,
        old_masked,
        projected,
        image_proj,
        image_old,
        last_proj,
        last_old,
    )


def solution(mesh):
    placed = (
        P(AXES, None, None),
        P(AXES, None, None),
        P(AXES, None, None),
        P(),
        P(AXES, None),
        P(AXES, None, None),
        P(AXES, None, None),
        P(AXES, None),
    )
    return jax.shard_map(
        on_device,
        mesh=mesh,
        in_specs=placed,
        out_specs=(P(AXES, None, None),) * 3,
        check_vma=False,
    )
```

```python
import functools

import jax
import jax.numpy as jnp
from jax import lax
from jax.experimental import pallas as pl
from jax.experimental.pallas import tpu as pltpu
from jax.sharding import PartitionSpec as P

AXES = ("sub", "grp")
HIGHEST = lax.Precision.HIGHEST
VMEM = pl.BlockSpec(memory_space=pltpu.VMEM)
HBM = pl.BlockSpec(memory_space=pltpu.HBM)
BLOCK = 256
ANY = pl.BlockSpec(memory_space=pl.ANY)
PARAMS = pltpu.CompilerParams(vmem_limit_bytes=8 << 20)


def shifted(block, distance):
    devices = range(lax.axis_size(AXES))
    route = [(i - distance, i) for i in devices if i - distance in devices]
    return lax.ppermute(block, AXES, route)


def swapped(block, distance):
    route = [(i, i ^ distance) for i in range(lax.axis_size(AXES))]
    return lax.ppermute(block, AXES, route)


def rows_dot(first, second, precision=None):
    return lax.dot_general(
        first,
        second,
        (((1,), (1,)), ((), ())),
        precision=precision,
        preferred_element_type=jnp.float32,
    )


def plain_dot(first, second, precision=None):
    return lax.dot_general(
        first,
        second,
        (((1,), (0,)), ((), ())),
        precision=precision,
        preferred_element_type=jnp.float32,
    )


def halves(values):
    high = values.astype(jnp.bfloat16)
    low = (values - high.astype(jnp.float32)).astype(jnp.bfloat16)
    return high, low


def thirds(values):
    high = values.astype(jnp.bfloat16)
    rest = values - high.astype(jnp.float32)
    middle = rest.astype(jnp.bfloat16)
    low = (rest - middle.astype(jnp.float32)).astype(jnp.bfloat16)
    return high, middle, low


def match_table(row):
    width = row.shape[1]
    positions = lax.broadcasted_iota(jnp.int32, (width, width), 0)
    return (positions == row).astype(jnp.float32).astype(jnp.bfloat16)


def in_lane_block(values, lane_block, copies):
    cases = values.shape[1]
    wide = jnp.concatenate([values] * copies, axis=1)
    lanes = lax.broadcasted_iota(jnp.int32, wide.shape, 1)
    first = lane_block * cases
    inside = (lanes >= first) & (lanes < first + cases)
    return jnp.where(inside, wide, 0.0)


def first_kernel(modes_in, coarse_in, residual_in, old_in, pack_next, modes, coarse, arrived):
    ranks, count, full = modes_in.shape
    _, cases, half = residual_in.shape
    rows, width = coarse.shape
    last = count - 1
    pairs = [
        (modes_in.at[:, :, pl.ds(half, half)], modes),
        (coarse_in.at[pl.ds(coarse_in.shape[0] - rows, rows)], coarse),
        (residual_in.at[last], pack_next.at[pl.ds(0, cases)]),
        (old_in.at[last], pack_next.at[pl.ds(cases, cases)]),
    ]
    fetches = [pltpu.make_async_copy(a, b, arrived.at[i]) for i, (a, b) in enumerate(pairs)]
    for fetch in fetches:
        fetch.start()
    row = 2 * cases
    pack_next[row:, :] = jnp.zeros((pack_next.shape[0] - row, half), jnp.float32)
    fetches[0].wait()
    pack_next[row : row + ranks, :] = modes[:, last, :]
    fetches[1].wait()
    for lane in range(0, width, half):
        row += 8
        part = coarse[rows - ranks :, lane : min(lane + half, width)]
        pack_next[row : row + ranks, : part.shape[1]] = part
    fetches[2].wait()
    fetches[3].wait()


def at_face_before(left, table):
    high, middle, low = thirds(left)
    stacked = jnp.concatenate(
        [high.astype(jnp.float32), middle.astype(jnp.float32), low.astype(jnp.float32), left * 0.0],
        axis=0,
    ).astype(jnp.bfloat16)
    moved = rows_dot(stacked, table)
    return moved[0:8] + moved[8:16] + moved[16:24]


def prepare_kernel(
    copies,
    share,
    matching_in,
    modes_in,
    coarse_in,
    residual_in,
    old_in,
    factor_in,
    face_modes,
    own_sums,
    pack_before,
    masked,
    old_masked,
    padded,
    matching,
    coarse_rows,
    *others,
):
    held, (modes, coarse, arrived) = others[:-3], others[-3:]
    count, cases, half = residual_in.shape
    ranks = modes_in.shape[0]
    fetches = []

    def fetch(source, target):
        copy = pltpu.make_async_copy(source, target, arrived.at[len(fetches)])
        copy.start()
        fetches.append(copy)

    fetch(matching_in, matching)
    fetch(modes_in, modes)
    fetch(residual_in, masked)
    fetch(old_in, old_masked)
    fetch(coarse_in, coarse)
    for a, rows in enumerate(held):
        _, depth, width = rows.shape
        fetch(factor_in.at[:, pl.ds(a * depth, depth), pl.ds(0, width)], rows)
    me = lax.axis_index(AXES)
    keep = jnp.where(me == lax.axis_size(AXES) - 1, 0.0, 1.0)
    lane_block = me // share
    padded[...] = jnp.zeros_like(padded)
    coarse_rows[...] = jnp.zeros_like(coarse_rows)
    fetches[0].wait()
    fetches[1].wait()
    for g in range(count):
        padded[g, 0:ranks, :] = modes[:, g, :]
    for g in range(count):
        face_modes[g] = at_face_before(padded[g, :, :half], match_table(matching[g : g + 1, :]))
    fetches[2].wait()
    masked[count - 1] = masked[count - 1] * keep
    sums = [0.0] * count
    for g in range(count):
        if g == count - 1:
            sums[g] = sums[g] + rows_dot(padded[g, :, half:], masked[g], HIGHEST)
        else:
            both = jnp.concatenate([padded[g, :, half:], face_modes[g + 1]], axis=0)
            found = rows_dot(both, masked[g], HIGHEST)
            sums[g] = sums[g] + found[0:8]
            sums[g + 1] = -found[8:16]
    own_sums[...] = jnp.zeros_like(own_sums)
    for g in range(count):
        own_sums[g * ranks : (g + 1) * ranks, :] = in_lane_block(sums[g], lane_block, copies)[0:ranks]
    fetches[4].wait()
    for g in range(count):
        coarse_rows[8 * g : 8 * g + ranks, :] = coarse[g * ranks : (g + 1) * ranks, :]
    width = half + coarse_rows.shape[1]
    pack_before[:, :half] = face_modes[0]
    pack_before[:, half:width] = coarse_rows[0:8, :]
    pack_before[:, width : width + coarse_rows.shape[1]] = coarse_rows[8:16, :]
    pack_before[:, width + coarse_rows.shape[1] :] = jnp.zeros((8, half), jnp.float32)
    fetches[3].wait()
    old_masked[count - 1] = old_masked[count - 1] * keep
    for copy in fetches[5:]:
        copy.wait()


def cross_kernel(copies, share, ranks, own_sums, face_modes, from_before, order, out):
    lane_block = lax.axis_index(AXES) // share
    cases = out.shape[1] // copies
    cross = rows_dot(face_modes[0], from_before[0:cases], HIGHEST)
    out[...] = own_sums[...]
    out[0:ranks, :] = own_sums[0:ranks, :] - in_lane_block(cross, lane_block, copies)[0:ranks]


def inner_part(g, matching, padded, masked, old_masked, face_modes, held, from_before, from_next, operand):
    count, cases, half = masked.shape
    full = 2 * half
    block = full // len(held)
    rows = operand.shape[0] // 2
    me = lax.axis_index(AXES)
    q = 2 * cases
    zeros8 = jnp.zeros((8, half), jnp.float32)
    left_modes = padded[g, :, :half]
    right_modes = padded[g, :, half:]
    if g == 0:
        prior_res, prior_old = from_before[0:cases], from_before[cases : 2 * cases]
        prior_modes = from_before[2 * cases : 2 * cases + 8]
        left_modes = left_modes * jnp.where(me == 0, 0.0, 1.0)
    else:
        prior_modes = padded[g - 1, :, half:]
        prior_res, prior_old = masked[g - 1], old_masked[g - 1]
    if g == count - 1:
        keep = jnp.where(me == lax.axis_size(AXES) - 1, 0.0, 1.0)
        next_faces = from_next[:, :half] * keep
        right_modes = right_modes * keep
    else:
        next_faces = face_modes[g + 1]

    right = jnp.concatenate(
        [masked[g], old_masked[g], zeros8, right_modes, -next_faces, zeros8], axis=0
    )
    right_high, right_low = halves(right)
    operand[0:rows, half:] = right_high
    operand[rows:, half:] = right_low

    moving = jnp.concatenate([prior_res, prior_old, prior_modes, zeros8], axis=0)
    high, low = halves(-moving)
    moved = plain_dot(jnp.concatenate([high, low], axis=0), match_table(matching[g : g + 1, :]))
    part = moving.shape[0]
    own_high, own_low = halves(left_modes)
    own_high = own_high.astype(jnp.float32)
    own_low = own_low.astype(jnp.float32)
    operand[0:rows, :half] = jnp.concatenate(
        [moved[0 : q + 8], own_high, zeros8, zeros8], axis=0
    ).astype(jnp.bfloat16)
    operand[rows:, :half] = jnp.concatenate(
        [moved[part : part + q + 8], own_low, zeros8, zeros8], axis=0
    ).astype(jnp.bfloat16)

    pieces = []
    for a in range(len(held)):
        found = rows_dot(operand[:, : (a + 1) * block], held[a][g])
        pieces.append(found[0:rows] + found[rows:])
    return right, jnp.concatenate(pieces, axis=1)


def store_inner(slot, right, found, inner, basis):
    cases, half = inner.shape[1] // 2, right.shape[1]
    q = 2 * cases
    inner[slot] = found[0:q]
    wide = jnp.concatenate([right[q : q + 24], found[q : q + 24]], axis=1)
    basis[slot] = three_terms(wide)


def three_terms(wide):
    high, low = halves(wide)
    high = high.astype(jnp.float32)
    return jnp.concatenate(
        [high, low.astype(jnp.float32), high, jnp.zeros_like(wide[0:8])], axis=0
    ).astype(jnp.bfloat16)


def across(coeffs, terms):
    high, low = halves(coeffs)
    high = high.astype(jnp.float32)
    stacked = jnp.concatenate(
        [high, high, low.astype(jnp.float32), jnp.zeros_like(coeffs[0:8])], axis=0
    ).astype(jnp.bfloat16)
    return lax.dot_general(
        stacked, terms, (((0,), (0,)), ((), ())), preferred_element_type=jnp.float32
    )


def outer_part(g, found, matching, held):
    rows, full = found.shape
    half = full // 2
    block = full // len(held)
    high, low = halves(found)
    operand = jnp.concatenate([high, low], axis=0)
    pieces = [0.0] * len(held)
    for a in range(len(held)):
        part = plain_dot(operand[:, a * block : (a + 1) * block], held[a][g])
        part = part[0:rows] + part[rows:]
        for b in range(a + 1):
            pieces[b] = pieces[b] + part[:, b * block : (b + 1) * block]
    per_half = half // block
    left = jnp.concatenate(pieces[:per_half], axis=1)
    right = jnp.concatenate(pieces[per_half:], axis=1)
    high, low = halves(left)
    moved = rows_dot(jnp.concatenate([high, low], axis=0), match_table(matching[g : g + 1, :]))
    return moved[0:rows] + moved[rows:], right


def later_kernel(subs, order, matching, padded, masked, old_masked, face_modes, *others):
    halos = len(subs) == 1
    from_next = others[0] if halos else None
    held, (inner, basis, whole, operand) = others[halos:-4], others[-4:]
    operand[...] = jnp.zeros_like(operand)
    for slot, g in enumerate(subs):
        right, found = inner_part(
            g, matching, padded, masked, old_masked, face_modes, held, None, from_next, operand
        )
        store_inner(slot, right, found, inner, basis)
        whole[slot] = found


def start_kernel(order, matching, padded, masked, old_masked, face_modes, from_before, *others):
    held, (inner, basis, right_first, returned, returned_rest, operand) = others[:-6], others[-6:]
    operand[...] = jnp.zeros_like(operand)
    right, found = inner_part(
        0, matching, padded, masked, old_masked, face_modes, held, from_before, None, operand
    )
    store_inner(0, right, found, inner, basis)
    moved, solved = outer_part(0, found, matching, held)
    right_first[...] = solved
    cut = returned.shape[0]
    returned[...] = moved[0:cut]
    returned_rest[...] = jnp.zeros_like(returned_rest)
    returned_rest[0 : returned_rest.shape[0] - 8] = moved[cut : cut + returned_rest.shape[0] - 8]


def outer_kernel(order, matching, whole_middle, whole_last, right_first, coeffs, *others):
    held, (image_proj, image_old) = others[:-2], others[-2:]
    count, cases, half = image_proj.shape
    q = 2 * cases
    keep = jnp.where(lax.axis_index(AXES) == lax.axis_size(AXES) - 1, 0.0, 1.0)
    following = jnp.zeros((q + 24, half), jnp.float32)
    zeros8 = jnp.zeros((8, half), jnp.float32)
    for g in reversed(range(count)):
        if g:
            found = whole_last[0] if g == count - 1 else whole_middle[g - 1]
            moved, solved = outer_part(g, found, matching, held)
        else:
            solved = right_first[...]
        both = solved[0:q] - following[0:q]
        basis = jnp.concatenate([solved[q : q + 24], zeros8], axis=0) - jnp.concatenate(
            [zeros8, following[q : q + 24]], axis=0
        )
        if g == count - 1:
            both, basis = both * keep, basis * keep
        image_proj[g] = both[0:cases] - across(coeffs[8 * g : 8 * g + 32], three_terms(basis))
        image_old[g] = both[cases:]
        if g:
            following = moved


def add_kernel(offsets, own, *others):
    total = own[...]
    for k in range(len(offsets)):
        total = total + others[k][...]
    others[-1][...] = total


def place_kernel(offsets, distance, own, *others):
    out = others[-1]
    place = (lax.axis_index(AXES) // distance) % out.shape[1]
    out[:, pl.ds(place, 1)] = own[...][:, None]
    for k, offset in enumerate(offsets):
        out[:, pl.ds(place ^ offset, 1)] = others[k][...][:, None]


def combine_kernel(
    copies,
    gathered,
    from_before,
    coarse_rows,
    from_next,
    masked,
    *others,
):
    parts, (projected, coeffs, sums) = others[:-3], others[-3:]
    count, cases, half = masked.shape
    width = coarse_rows.shape[1]
    own = gathered[...].reshape(gathered.shape[0] * gathered.shape[1], copies * cases)
    stacked = jnp.concatenate([own[:, b * cases : (b + 1) * cases] for b in range(copies)], axis=0)
    first = 2 * cases + 8
    prior = jnp.concatenate(
        [from_before[k : k + 8] for k in range(first, from_before.shape[0], 8)], axis=1
    )
    rows = jnp.concatenate(
        [
            prior[:, :width],
            coarse_rows[...],
            from_next[:, half : half + width],
            from_next[:, half + width : half + 2 * width],
        ],
        axis=0,
    )
    high, low = halves(rows)
    stacked_high, stacked_low = halves(stacked)
    depth = rows.shape[0]
    wide = plain_dot(
        jnp.concatenate([high.astype(jnp.float32), low.astype(jnp.float32)], axis=0).astype(
            jnp.bfloat16
        ),
        stacked_high,
    )
    near = wide[0:depth] + wide[depth:] + plain_dot(high, stacked_low)
    coeffs[...] = near
    lanes = 128
    totals = [jnp.zeros((cases, lanes), jnp.float32) for _ in range(4)]

    def folded(values):
        out = values[:, :lanes]
        for k in range(1, values.shape[1] // lanes):
            out = out + values[:, k * lanes : (k + 1) * lanes]
        return out

    for g in range(count):
        place = 0 if g == 0 else 4 if g == count - 1 else 2
        slot = g - 1 if place == 2 else 0
        inner = parts[place][slot]
        spread = across(near[8 * g : 8 * g + 24], parts[place + 1][slot])
        proj = masked[g] - spread[:, :half]
        mine = inner[0:cases] - spread[:, half:]
        other = inner[cases:]
        projected[g] = proj
        totals[0] += folded(proj * proj)
        totals[1] += folded(mine * mine)
        totals[2] += folded(mine * other)
        totals[3] += folded(other * other)
    high, low = halves(jnp.concatenate(totals, axis=0))
    ones = jnp.ones((8, lanes), jnp.bfloat16)
    sums[...] = rows_dot(ones, high) + rows_dot(ones, low)


def settle_kernel(order, image_proj, image_old, coeffs, received_first, received_rest, proj, old):
    count, cases, _ = image_proj.shape
    received = jnp.concatenate([received_first[...], received_rest[...]], axis=0)
    basis = three_terms(received[2 * cases : 2 * cases + 24])
    near = coeffs[8 * count : 8 * count + 24]
    proj[...] = image_proj[count - 1] - received[0:cases] + across(near, basis)
    old[...] = image_old[count - 1] - received[cases : 2 * cases]


def finish_kernel(
    sums,
    old_norms,
    multipliers,
    masked,
    old_masked,
    projected,
    image_proj,
    image_old,
    last_proj,
    last_old,
    new_multipliers,
    new_residual,
    direction,
):
    count, cases, half = masked.shape
    diagonal = lax.broadcasted_iota(jnp.int32, (cases, cases), 0) == lax.broadcasted_iota(
        jnp.int32, (cases, cases), 1
    )

    def column(row):
        return jnp.sum(jnp.where(diagonal, row, 0.0), axis=1, keepdims=True)

    norms = sums[0:1, 0:cases]
    ratio = norms / old_norms[...]
    curvature = (
        sums[0:1, cases : 2 * cases]
        + 2.0 * ratio * sums[0:1, 2 * cases : 3 * cases]
        + ratio * ratio * sums[0:1, 3 * cases : 4 * cases]
    )
    step_len = column(norms / curvature)
    ratio = column(ratio)
    for g in range(count):
        image_p, image_o = image_proj[g], image_old[g]
        if g == count - 1:
            image_p, image_o = last_proj[...], last_old[...]
        towards = projected[g] + ratio * old_masked[g]
        direction[g] = towards
        new_multipliers[g] = multipliers[g] + step_len * towards
        new_residual[g] = masked[g] - step_len * (image_p + ratio * image_o)


def on_device(
    multipliers,
    residual,
    old_direction,
    old_norms,
    matching,
    factor_inverse,
    rigid_modes,
    coarse_inverse,
):
    count, cases, half = residual.shape
    ranks = rigid_modes.shape[1]
    full = factor_inverse.shape[1]
    own_rows, coarse_width = coarse_inverse.shape
    devices = lax.axis_size(AXES)
    copies = min(128 // cases, devices)
    share = devices // copies
    f32 = jnp.float32
    shape = jax.ShapeDtypeStruct
    row_block = min(BLOCK, full)
    row_blocks = full // row_block
    q = 2 * cases
    cut = q - 8
    in_hbm = lambda *arrays: (pltpu.with_memory_space_constraint(x, pltpu.HBM) for x in arrays)

    modes_by_rank = rigid_modes.transpose(1, 0, 2)
    next_rows = 2 * cases + 8 + 8 * pl.cdiv(coarse_width, half)
    coarse_part = own_rows - (own_rows - ranks) // 8 * 8
    pack_next = pl.pallas_call(
        first_kernel,
        out_shape=shape((next_rows, half), f32),
        in_specs=[HBM] * 4,
        out_specs=VMEM,
        scratch_shapes=[
            pltpu.VMEM((ranks, count, half), f32),
            pltpu.VMEM((coarse_part, coarse_width), f32),
            pltpu.SemaphoreType.DMA((4,)),
        ],
        compiler_params=PARAMS,
        name="first",
    )(*in_hbm(modes_by_rank, coarse_inverse, residual, old_direction))

    from_before = shifted(pack_next, 1)

    (
        face_modes,
        own_sums,
        pack_before,
        masked,
        old_masked,
        padded,
        match_copy,
        coarse_rows,
        *factor,
    ) = pl.pallas_call(
        functools.partial(prepare_kernel, copies, share),
        out_shape=(
            shape((count, 8, half), f32),
            shape((own_rows, copies * cases), f32),
            shape((8, 2 * half + 2 * coarse_width), f32),
            shape((count, cases, half), f32),
            shape((count, cases, half), f32),
            shape((count, 8, full), f32),
            shape((count, half), jnp.int32),
            shape((8 * count, coarse_width), f32),
        )
        + tuple(
            shape((count, row_block, (a + 1) * row_block), jnp.bfloat16) for a in range(row_blocks)
        ),
        in_specs=[HBM] * 6,
        out_specs=(VMEM,) * (8 + row_blocks),
        scratch_shapes=[
            pltpu.VMEM((ranks, count, full), f32),
            pltpu.VMEM((own_rows, coarse_width), f32),
            pltpu.SemaphoreType.DMA((5 + row_blocks,)),
        ],
        compiler_params=PARAMS,
        name="prepare",
    )(
        *in_hbm(
            matching, modes_by_rank, coarse_inverse, residual, old_direction, factor_inverse
        )
    )

    from_next = shifted(pack_before, -1)

    operand = pltpu.VMEM((2 * (q + 32), full), jnp.bfloat16)
    fields = (match_copy, padded, masked, old_masked, face_modes)

    def exchanged(block, distance, width, placed, *after):
        offsets = tuple(range(1, width))
        partners = [swapped(block, k * distance) for k in offsets]
        size = block.shape
        if placed:
            kernel = functools.partial(place_kernel, offsets, distance)
            size = (block.shape[0], width) + block.shape[1:]
        else:
            kernel = functools.partial(add_kernel, offsets)
        return pl.pallas_call(
            kernel,
            out_shape=shape(size, f32),
            in_specs=[VMEM] * width + [ANY] * len(after),
            out_specs=VMEM,
            compiler_params=PARAMS,
            name="merge",
        )(block, *partners, *after)

    def rounds_of(most):
        rounds = []
        distance = devices
        while distance > 1:
            width = most if 2 * most <= distance <= share else 2
            distance //= width
            rounds.append((distance, width))
        return rounds

    rounds = rounds_of(2)
    lane_rounds = [one for one in rounds if one[0] >= share]
    rounds = lane_rounds[::-1] + rounds[len(lane_rounds) :]

    def inner(subs, order, *halos):
        return pl.pallas_call(
            functools.partial(later_kernel, subs),
            out_shape=(
                shape((len(subs), q, full), f32),
                shape((len(subs), 80, half + full), jnp.bfloat16),
                shape((len(subs), q + 32, full), f32),
            ),
            in_specs=[ANY] + [VMEM] * (5 + len(halos) + row_blocks),
            out_specs=(VMEM,) * 3,
            scratch_shapes=[operand],
            compiler_params=PARAMS,
            name="inner_last" if halos else "inner_middle",
        )(order, *fields, *halos, *factor)

    inner_middle, basis_middle, whole_middle = inner(tuple(range(1, count - 1)), own_sums)
    block = pl.pallas_call(
        functools.partial(cross_kernel, copies, share, ranks),
        out_shape=shape((own_rows, copies * cases), f32),
        in_specs=[VMEM] * 3 + [ANY],
        out_specs=VMEM,
        compiler_params=PARAMS,
        name="cross",
    )(own_sums, face_modes, from_before, whole_middle)

    for turn, (distance, width) in enumerate(rounds):
        after = ()
        if turn == 0:
            inner_first, basis_first, right_first, *returned = pl.pallas_call(
                start_kernel,
                out_shape=(
                    shape((1, q, full), f32),
                    shape((1, 80, half + full), jnp.bfloat16),
                    shape((q + 32, half), f32),
                    shape((cut, half), f32),
                    shape((q + 24 + 8 - cut, half), f32),
                ),
                in_specs=[ANY] + [VMEM] * (6 + row_blocks),
                out_specs=(VMEM,) * 5,
                scratch_shapes=[operand],
                compiler_params=PARAMS,
                name="inner_first",
            )(block, *fields, from_before, *factor)
            after = (returned[0],)
            received = [shifted(part, -1) for part in returned]
        elif turn == len(rounds) - 1:
            inner_last, basis_last, whole_last = inner((count - 1,), block, from_next)
            after = (whole_last,)
        placed = distance < share
        if placed and block.ndim == 2:
            block = block[None]
        block = exchanged(block, distance, width, placed, *after)
        if placed:
            block = block.reshape((-1,) + block.shape[2:])

    projected, coeffs, sums = pl.pallas_call(
        functools.partial(combine_kernel, copies),
        out_shape=(
            shape((count, cases, half), f32),
            shape((8 * (count + 3), cases), f32),
            shape((8, 4 * cases), f32),
        ),
        in_specs=[VMEM] * 11,
        out_specs=(VMEM,) * 3,
        compiler_params=PARAMS,
        name="combine",
    )(
        block,
        from_before,
        coarse_rows,
        from_next,
        masked,
        inner_first,
        basis_first,
        inner_middle,
        basis_middle,
        inner_last,
        basis_last,
    )

    image_proj, image_old = pl.pallas_call(
        outer_kernel,
        out_shape=(shape((count, cases, half), f32),) * 2,
        in_specs=[ANY] + [VMEM] * (5 + row_blocks),
        out_specs=(VMEM,) * 2,
        compiler_params=PARAMS,
        name="outer",
    )(sums, match_copy, whole_middle, whole_last, right_first, coeffs, *factor)
    after = (image_proj,)
    rounds = sorted(rounds_of(4), key=lambda one: -one[1])
    for distance, width in rounds:
        if distance == rounds[-1][0]:
            last_proj, last_old = pl.pallas_call(
                settle_kernel,
                out_shape=(shape((cases, half), f32),) * 2,
                in_specs=[ANY] + [VMEM] * 5,
                out_specs=(VMEM,) * 2,
                compiler_params=PARAMS,
                name="settle",
            )(sums, image_proj, image_old, coeffs, *received)
            after = (last_proj,)
        sums = exchanged(sums, distance, width, False, *after)
        after = ()

    return pl.pallas_call(
        finish_kernel,
        out_shape=(shape((count, cases, half), f32),) * 3,
        in_specs=[VMEM] * 10,
        out_specs=(VMEM,) * 3,
        compiler_params=PARAMS,
        name="finish",
    )(
        sums,
        old_norms.reshape(1, cases),
        multipliers,
        masked,
        old_masked,
        projected,
        image_proj,
        image_old,
        last_proj,
        last_old,
    )


def solution(mesh):
    placed = (
        P(AXES, None, None),
        P(AXES, None, None),
        P(AXES, None, None),
        P(),
        P(AXES, None),
        P(AXES, None, None),
        P(AXES, None, None),
        P(AXES, None),
    )
    return jax.shard_map(
        on_device,
        mesh=mesh,
        in_specs=placed,
        out_specs=(P(AXES, None, None),) * 3,
        check_vma=False,
    )
```
